256 devices in a mesh: pb: 8 (over z_hi, core), ka: 32 (over y, x, z_lo).
Axes of the slice: x: 4, y: 4, z: 8 (z_hi: 4, z_lo: 2; z = z_hi * 2 + z_lo), core: 2. Of those that a mesh axis runs over, the one named last changes fastest.
Arguments:
- queries: bfloat16 [40960, 128], P(('pb', 'ka')), may hold values from -6 to 6
- keys_in: bfloat16 [40960, 128], P(('pb', 'ka')), may hold values from -6 to 6
- values_in: bfloat16 [40960, 128], P(('pb', 'ka')), may hold values from -6 to 6
- outputs_saved: bfloat16 [40960, 128], P(('pb', 'ka')), may hold values from -6 to 6
- out_grad: bfloat16 [40960, 128], P(('pb', 'ka')), may hold values from -24 to 24
- log_sum: float32 [40960], P(('pb', 'ka'))
- block_table: int32 [512], replicated, may hold values from 0 to 511, as said below
Outputs:
- grad_queries: bfloat16 [40960, 128], P(('pb', 'ka'))
- grad_keys: bfloat16 [40960, 128], P(('pb', 'ka'))
- grad_values: bfloat16 [40960, 128], P(('pb', 'ka'))
The draws below stay inside these ranges and needn't reach their ends.
Inputs may be any that keep to these rules, and one draw needn't show every extreme that they name: block_table is a permutation: storage block b holds the segment's tokens 80 * block_table[b] to 80 * block_table[b] + 79.
All inputs are finite; a program needn't handle non-finite values.
Results may differ from the reference program's by a relative error of at most 0.0069.
Values may be sent and summed in bfloat16 or wider, within the bound.
A program may use at most 64 MiB of HBM per device.

```python
import jax
import jax.numpy as jnp
from jax import lax

HEAD = 128
BLK = 80
NBLK = 512
SEQ = 40960


def block_order(key):
    return jax.random.permutation(key, NBLK).astype(jnp.int32)


def draw_block_table(key, part):
    return block_order(key)


def draw_log_sum(key, part):
    order = block_order(key)
    key = jax.random.fold_in(key, 7)
    offsets = jnp.arange(BLK, dtype=jnp.int32)
    position = (order[:, None] * BLK + offsets[None, :]).reshape(-1).astype(jnp.float32)
    noise = jax.random.uniform(key, (SEQ,), jnp.float32, -0.3, 0.3)
    return jnp.log(position + 1.0) + 0.5 + noise


def level_of(own_key, extent, pieces, least, top_value):
    def one(dim, shards_of):
        heights = jax.random.uniform(jax.random.fold_in(jax.random.fold_in(own_key, 6), dim), (shards_of,), jnp.float32, least / len(pieces), top_value / len(pieces))
        return jnp.repeat(jnp.exp(heights), extent[dim] // shards_of).reshape((-1,) + (1,) * (len(extent) - dim - 1))

    factor_of = one(*pieces[0])
    for cut in pieces[1:]:
        factor_of = factor_of * one(*cut)
    return factor_of


def scatter_about(own_key, shape, deviation, most, cuts=(), kind=jnp.bfloat16):
    array = jax.random.normal(own_key, shape, jnp.float32) * deviation
    if len(cuts) > 0:
        array = level_of(own_key, shape, cuts, -0.22, 0.18) * array
    return jnp.clip(array, min=-most, max=most).astype(kind)


def setup_inputs(seed: int = 0) -> dict:
    seeds = jax.random.split(jax.random.key(seed), 8)
    return {
        "queries": scatter_about(seeds[0], (SEQ, HEAD), 1.0, 6.0, ((0, 256),)),
        "keys_in": scatter_about(seeds[1], (SEQ, HEAD), 1.0, 6.0, ((0, 256),)),
        "values_in": scatter_about(seeds[2], (SEQ, HEAD), 1.0, 6.0, ((0, 256),)),
        "outputs_saved": scatter_about(seeds[3], (SEQ, HEAD), 1.0, 6.0, ((0, 256),)),
        "out_grad": scatter_about(seeds[4], (SEQ, HEAD), 4.0, 24.0, ((0, 256),)),
        "log_sum": draw_log_sum(jax.random.fold_in(seeds[7], 71), 0),
        "block_table": draw_block_table(jax.random.fold_in(seeds[7], 71), 0),
    }


def reference(queries, keys_in, values_in, outputs_saved, out_grad, log_sum, block_table):
    total = queries.shape[0]
    width = queries.shape[1]
    scale = 1.0 / (width ** 0.5)
    offsets = jnp.arange(BLK, dtype=jnp.int32)
    position = (block_table[:, None] * BLK + offsets[None, :]).reshape(-1).astype(jnp.int32)
    delta = jnp.sum(out_grad.astype(jnp.float32) * outputs_saved.astype(jnp.float32), axis=1)
    rows_blk = 8 * BLK
    count = total // rows_blk
    q_blocks = queries.reshape(count, rows_blk, width)
    g_blocks = out_grad.reshape(count, rows_blk, width)
    l_blocks = log_sum.reshape(count, rows_blk)
    d_blocks = delta.reshape(count, rows_blk)
    p_blocks = position.reshape(count, rows_blk)

    def step(carry, item):
        grad_k, grad_v = carry
        q_b, g_b, l_b, d_b, pos_b = item
        scores = lax.dot_general(q_b, keys_in, (((1,), (1,)), ((), ())), preferred_element_type=jnp.float32) * scale
        visible = pos_b[:, None] >= position[None, :]
        probs = jnp.where(visible, jnp.exp(scores - l_b[:, None]), 0.0)
        dprobs = lax.dot_general(g_b, values_in, (((1,), (1,)), ((), ())), preferred_element_type=jnp.float32)
        dscores = (probs * (dprobs - d_b[:, None]) * scale).astype(jnp.bfloat16)
        probs_b = probs.astype(jnp.bfloat16)
        grad_v = grad_v + lax.dot_general(probs_b, g_b, (((0,), (0,)), ((), ())), preferred_element_type=jnp.float32)
        grad_k = grad_k + lax.dot_general(dscores, q_b, (((0,), (0,)), ((), ())), preferred_element_type=jnp.float32)
        grad_q = jnp.dot(dscores, keys_in, preferred_element_type=jnp.float32)
        return (grad_k, grad_v), grad_q

    zeros = jnp.zeros((total, width), jnp.float32)
    (grad_k, grad_v), grad_q = lax.scan(step, (zeros, zeros), (q_blocks, g_blocks, l_blocks, d_blocks, p_blocks))
    grad_q = grad_q.reshape(total, width)
    return grad_q.astype(jnp.bfloat16), grad_k.astype(jnp.bfloat16), grad_v.astype(jnp.bfloat16)
```

```python
import math

import jax
import jax.numpy as jnp
from jax import lax
from jax.experimental import pallas as pl
from jax.experimental.pallas import tpu as pltpu
from jax.sharding import PartitionSpec as P

MESH = pl.DeviceIdType.MESH
F32, BF16 = jnp.float32, jnp.bfloat16
ROWS = 160
BLK = 80
WIDTH = 128
SCALE = 1.0 / math.sqrt(WIDTH)
TO_EXP2 = SCALE * math.log2(math.e)
LOG2E = math.log2(math.e)
HIDDEN = 1e30
CHUNK = 336
PLANE = (
    (0, 0), (1, 0), (3, 0), (0, 1), (0, 3), (1, 1), (3, 3), (1, 3),
    (3, 1), (2, 0), (0, 2), (2, 1), (2, 3), (1, 2), (3, 2), (2, 2),
)
LINE = (0, 1, 7, 2, 6, 3, 5, 4)
Q_TILE, K_TILE = 8 * ROWS, 4 * ROWS
NT = (((1,), (1,)), ((), ()))
TN = (((0,), (0,)), ((), ()))


def plane_slot(dx, dy):
    return PLANE.index((dx % 4, dy % 4))


def line_slot(dz):
    return LINE.index(dz % 8)


def place():
    pb, ka = lax.axis_index("pb"), lax.axis_index("ka")
    x, y, z, c = (ka // 2) % 4, ka // 8, (pb // 2) * 2 + ka % 2, pb % 2
    return x, y, z, c


def device(x, y, z, c):
    return ((z // 2) * 2 + c, y * 8 + x * 2 + z % 2)


def storage(x, y, z, c):
    pb, ka = device(x, y, z, c)
    return pb * 32 + ka


def kernel(
    q_in, k_in, v_in, o_in, g_in, l_in, table,
    dq_out, dk_out, dv_out,
    qg, kv, o_own, dq_acc, dk_acc, dv_acc, lrow, drow, keyid,
    dq_send, dq_recv, sib_send, sib_recv, dkv_send, dkv_recv, dkv_cross,
    local_sem, q_ss, q_rs, kz_ss, kz_rs, kc_ss, kc_rs,
    dq_ss, dq_rs, sib_ss, sib_rs, dkv_ss, dkv_rs, cross_ss, cross_rs,
):
    x, y, z, c = place()
    other = 1 - c

    def plane_dev(i):
        dx, dy = PLANE[i]
        return device((x + dx) % 4, (y + dy) % 4, z, c)

    def line_dev(i):
        return device(x, y, (z + LINE[i]) % 8, c)

    sibling = device(x, y, z, other)
    cross_up = device(x, y, (z + 1) % 8, other)
    cross_down = device(x, y, (z + 7) % 8, other)
    partners = [plane_dev(i) for i in range(1, 16)]
    partners += [line_dev(i) for i in range(1, 8)]
    partners += [sibling, cross_up, cross_down]
    barrier = pltpu.get_barrier_semaphore()
    for p in partners:
        pl.semaphore_signal(barrier, inc=1, device_id=p, device_id_type=MESH)

    loads = [
        pltpu.make_async_copy(g_in, qg.at[0, pl.ds(ROWS, ROWS)], local_sem.at[0]),
        pltpu.make_async_copy(o_in, o_own, local_sem.at[1]),
        pltpu.make_async_copy(q_in, qg.at[0, pl.ds(0, ROWS)], local_sem.at[2]),
        pltpu.make_async_copy(k_in, kv.at[0, 0, 0], local_sem.at[3]),
        pltpu.make_async_copy(v_in, kv.at[1, 0, 0], local_sem.at[4]),
    ]
    for cp in loads:
        cp.start()
    dq_acc[...] = jnp.zeros_like(dq_acc)
    dk_acc[...] = jnp.zeros_like(dk_acc)
    dv_acc[...] = jnp.zeros_like(dv_acc)
    for cp in loads:
        cp.wait()

    q0, g0 = qg[0, 0:ROWS, :], qg[0, ROWS : 2 * ROWS, :]
    k0, v0 = kv[0, 0, 0], kv[1, 0, 0]
    prod = g0.astype(F32) * o_own[...].astype(F32)
    high = prod.astype(BF16)
    low = (prod - high.astype(F32)).astype(BF16)
    ones = jnp.ones((8, WIDTH), BF16)
    delta8 = lax.dot_general(ones, high, NT, preferred_element_type=F32)
    delta8 += lax.dot_general(ones, low, NT, preferred_element_type=F32)
    delta = delta8[0:1, :]
    lse = l_in[...] * LOG2E
    sub = lax.broadcasted_iota(jnp.int32, (8, ROWS), 0)
    both = jnp.where(sub % 2 == 0, lse, delta)
    p1 = both.astype(BF16).astype(F32)
    p2 = (both - p1).astype(BF16).astype(F32)
    p3 = both - p1 - p2
    pieces = jnp.where(sub < 2, p1, jnp.where(sub < 4, p2, jnp.where(sub < 6, p3, 0.0)))
    wide = jnp.concatenate([pieces, jnp.zeros((8, 256 - ROWS), F32)], axis=1)
    first, rest = wide[:, 0:128], wide[:, 128:256]
    lane = lax.broadcasted_iota(jnp.int32, (8, 128), 1)
    second = jnp.where(
        lane < 48, pltpu.roll(first, 48, 1), pltpu.roll(rest, 48, 1)
    )
    keep = lane < BLK
    stats = jnp.concatenate(
        [jnp.where(keep, first, 0.0), jnp.where(keep, second, 0.0)], axis=0
    )
    qg[0, 2 * ROWS : CHUNK, :] = stats.astype(BF16)

    pl.semaphore_wait(barrier, len(partners))

    q_cps, kz_cps = {}, {}
    for i in range(1, 16):
        dx, dy = PLANE[i]
        q_cps[i] = pltpu.make_async_remote_copy(
            src_ref=qg.at[0], dst_ref=qg.at[plane_slot(-dx, -dy)],
            send_sem=q_ss.at[i], recv_sem=q_rs.at[plane_slot(-dx, -dy)],
            device_id=plane_dev(i), device_id_type=MESH,
        )
    for i in range(1, 8):
        to = line_slot(-LINE[i])
        kz_cps[i] = pltpu.make_async_remote_copy(
            src_ref=kv.at[:, 0, 0], dst_ref=kv.at[:, to, 0],
            send_sem=kz_ss.at[i], recv_sem=kz_rs.at[to],
            device_id=line_dev(i), device_id_type=MESH,
        )
    kc_cps = [
        pltpu.make_async_remote_copy(
            src_ref=kv.at[:, s, 0], dst_ref=kv.at[:, s, 1],
            send_sem=kc_ss.at[s], recv_sem=kc_rs.at[s],
            device_id=sibling, device_id_type=MESH,
        )
        for s in range(8)
    ]
    kc_cps[0].start()
    for i in (1, 2):
        kz_cps[i].start()
    for i in range(1, 5):
        q_cps[i].start()
    for i in (3, 4):
        kz_cps[i].start()
    for i in range(5, 9):
        q_cps[i].start()
    for i in (5, 6, 7):
        kz_cps[i].start()
    for i in range(9, 16):
        q_cps[i].start()

    def q_arrived(i):
        dx, dy = PLANE[i]
        q_cps[plane_slot(-dx, -dy)].wait_recv()

    def kz_arrived(s):
        kz_cps[line_slot(-LINE[s])].wait_recv()

    row = lax.broadcasted_iota(jnp.int32, (ROWS, ROWS), 0)
    col = lax.broadcasted_iota(jnp.int32, (ROWS, ROWS), 1)
    seen = (row <= col) & ((row >= BLK) == (col >= BLK))
    s0 = lax.dot_general(k0, q0, NT, preferred_element_type=F32)
    e0 = jnp.exp2(jnp.where(seen, s0 * TO_EXP2 - lse, -HIDDEN))
    dp0 = lax.dot_general(v0, g0, NT, preferred_element_type=F32)
    ds0 = (e0 * (dp0 - delta)).astype(BF16)
    dq_acc[0:ROWS, :] = lax.dot_general(ds0, k0, TN, preferred_element_type=F32)
    dk_acc[0:ROWS, :] = jnp.dot(ds0, q0, preferred_element_type=F32)
    dv_acc[0:ROWS, :] = jnp.dot(e0.astype(BF16), g0, preferred_element_type=F32)

    for r in range(32):
        s, h, b = r // 4, (r % 4) // 2, r % 2
        at = storage(x, y, (z + LINE[s]) % 8, c if h == 0 else other) * 2 + b
        keyid[r : r + 1, :] = jnp.full((1, 128), table[at], jnp.int32)

    def rows_of(half):
        blocks = []
        for i in range(8 * half, 8 * half + 8):
            st = qg[i, 2 * ROWS : CHUNK, :].astype(F32)
            dx, dy = PLANE[i]
            at = storage((x + dx) % 4, (y + dy) % 4, z, c) * 2
            blocks += [(st[0:8, :], table[at]), (st[8:16, :], table[at + 1])]
        for j in range(10):
            acc = jnp.zeros((8, 128), F32)
            ids = jnp.zeros((8, 128), jnp.int32)
            for r, (st, entry) in enumerate(blocks):
                shift = BLK * r - 128 * j
                if shift <= -BLK or shift >= 128:
                    continue
                here = (lane >= max(shift, 0)) & (lane < min(128, shift + BLK))
                moved = st if shift % 128 == 0 else pltpu.roll(st, shift % 128, 1)
                acc = jnp.where(here, moved, acc)
                ids = jnp.where(here, entry, ids)
            lr = acc[0:1, :] + acc[2:3, :] + acc[4:5, :]
            dr = acc[1:2, :] + acc[3:4, :] + acc[5:6, :]
            cols = slice(Q_TILE * half + 128 * j, Q_TILE * half + 128 * (j + 1))
            drow[:, cols] = jnp.broadcast_to(dr, (8, 128))
            lb = jnp.broadcast_to(lr, (8, 128))
            for t in range(4):
                lrow[8 * t : 8 * t + 8, cols] = jnp.where(
                    ids > keyid[8 * t : 8 * t + 8, :], lb, HIDDEN
                )

    def tile(qi, ki):
        qs = pl.ds(pl.multiple_of(qi * Q_TILE, Q_TILE), Q_TILE)
        ks = pl.ds(pl.multiple_of(ki * K_TILE, K_TILE), K_TILE)
        q = qg[pl.ds(qi * 8, 8), 0:ROWS, :].reshape(Q_TILE, WIDTH)
        g = qg[pl.ds(qi * 8, 8), ROWS : 2 * ROWS, :].reshape(Q_TILE, WIDTH)
        k = kv[0, pl.ds(ki * 2, 2), :, :, :].reshape(K_TILE, WIDTH)
        v = kv[1, pl.ds(ki * 2, 2), :, :, :].reshape(K_TILE, WIDTH)
        s = lax.dot_general(k, q, NT, preferred_element_type=F32)
        dp = lax.dot_general(v, g, NT, preferred_element_type=F32)
        lr = lrow[pl.ds(pl.multiple_of(ki * 8, 8), 8), qs]
        bias = jnp.broadcast_to(lr[:, None, :], (8, BLK, Q_TILE)).reshape(K_TILE, Q_TILE)
        p = jnp.exp2(s * TO_EXP2 - bias)
        ds = (p * (dp - drow[0:1, qs])).astype(BF16)
        dv_acc[ks, :] += jnp.dot(p.astype(BF16), g, preferred_element_type=F32)
        dk_acc[ks, :] += jnp.dot(ds, q, preferred_element_type=F32)
        dq_acc[qs, :] += lax.dot_general(ds, k, TN, preferred_element_type=F32)

    dq_cps, sib_cps, dkv_cps = {}, {}, {}
    for i in range(1, 16):
        dx, dy = PLANE[i]
        dq_cps[i] = pltpu.make_async_remote_copy(
            src_ref=dq_send.at[i], dst_ref=dq_recv.at[plane_slot(-dx, -dy)],
            send_sem=dq_ss.at[i], recv_sem=dq_rs.at[plane_slot(-dx, -dy)],
            device_id=plane_dev(i), device_id_type=MESH,
        )
    for s in range(8):
        sib_cps[s] = pltpu.make_async_remote_copy(
            src_ref=sib_send.at[s], dst_ref=sib_recv.at[s],
            send_sem=sib_ss.at[s], recv_sem=sib_rs.at[s],
            device_id=sibling, device_id_type=MESH,
        )
        if s > 0:
            to = line_slot(-LINE[s])
            dkv_cps[s] = pltpu.make_async_remote_copy(
                src_ref=dkv_send.at[s], dst_ref=dkv_recv.at[to],
                send_sem=dkv_ss.at[s], recv_sem=dkv_rs.at[to],
                device_id=line_dev(s), device_id_type=MESH,
            )
    cross = pltpu.make_async_remote_copy(
        src_ref=sib_send.at[1], dst_ref=dkv_cross,
        send_sem=cross_ss, recv_sem=cross_rs,
        device_id=cross_up, device_id_type=MESH,
    )

    def dq_out_half(half):
        for i in range(8 * half, 8 * half + 8):
            if i > 0:
                dq_send[i] = dq_acc[i * ROWS : (i + 1) * ROWS, :].astype(BF16)
                dq_cps[i].start()

    def part(acc, s, h):
        at = s * 2 * ROWS + h * ROWS
        return acc[at : at + ROWS, :]

    def to_sibling(s):
        sib_send[s, 0] = part(dk_acc, s, 1).astype(BF16)
        sib_send[s, 1] = part(dv_acc, s, 1).astype(BF16)
        if s != 1:
            sib_cps[s].start()

    def to_owner(s):
        a, b = part(dk_acc, s, 0), part(dv_acc, s, 0)
        if s != 1:
            sib_cps[s].wait_recv()
            a = a + sib_recv[s, 0].astype(F32)
            b = b + sib_recv[s, 1].astype(F32)
        dkv_send[s, 0] = a.astype(BF16)
        dkv_send[s, 1] = b.astype(BF16)
        dkv_cps[s].start()

    def keys_arrived(group):
        for s in (2 * group, 2 * group + 1):
            if s > 0:
                kz_arrived(s)
                kc_cps[s].start()

    def step(n, carry):
        qi = n // 4
        ki = jnp.where(n < 4, n, 7 - n)

        @pl.when(n == 0)
        def _():
            keys_arrived(0)
            for i in range(1, 8):
                q_arrived(i)
            rows_of(0)

        for group in range(4):

            @pl.when(n == group)
            def _():
                if group > 0:
                    keys_arrived(group)
                for s in (2 * group, 2 * group + 1):
                    kc_cps[s].wait_recv()

        @pl.when(n == 4)
        def _():
            dq_out_half(0)
            for i in range(8, 16):
                q_arrived(i)
            rows_of(1)

        for group in (3, 2, 1):

            @pl.when(n == 8 - group)
            def _():
                for s in (2 * group, 2 * group + 1):
                    to_sibling(s)
                if group < 3:
                    for s in (2 * group + 2, 2 * group + 3):
                        to_owner(s)

        tile(qi, ki)
        return carry

    lax.fori_loop(0, 8, step, 0)

    to_sibling(1)
    cross.start()
    to_owner(1)
    to_sibling(0)
    dq_out_half(1)
    for s in (2, 3):
        to_owner(s)

    total = dq_acc[0:ROWS, :]
    for i in range(1, 16):
        dx, dy = PLANE[i]
        dq_cps[plane_slot(-dx, -dy)].wait_recv()
        total = total + dq_recv[i].astype(F32)
    dq_out[...] = (total * SCALE).astype(BF16)
    a, b = part(dk_acc, 0, 0), part(dv_acc, 0, 0)
    sib_cps[0].wait_recv()
    a, b = a + sib_recv[0, 0].astype(F32), b + sib_recv[0, 1].astype(F32)
    for s in range(1, 8):
        dkv_cps[line_slot(-LINE[s])].wait_recv()
        a, b = a + dkv_recv[s, 0].astype(F32), b + dkv_recv[s, 1].astype(F32)
    cross.wait_recv()
    a, b = a + dkv_cross[0].astype(F32), b + dkv_cross[1].astype(F32)
    dk_out[...] = (a * SCALE).astype(BF16)
    dv_out[...] = b.astype(BF16)

    for group in (q_cps, kz_cps, dq_cps, dkv_cps):
        for cp in group.values():
            cp.wait_send()
    for s in range(8):
        kc_cps[s].wait_send()
        if s != 1:
            sib_cps[s].wait_send()
    cross.wait_send()


def per_device(queries, keys_in, values_in, outputs_saved, out_grad, log_sum, block_table):
    hbm = pl.BlockSpec(memory_space=pl.ANY)
    vmem = pl.BlockSpec(memory_space=pltpu.VMEM)
    smem = pl.BlockSpec(memory_space=pltpu.SMEM)
    dma = pltpu.SemaphoreType.DMA
    out = jax.ShapeDtypeStruct((ROWS, WIDTH), BF16)
    return pl.pallas_call(
        kernel,
        out_shape=(out, out, out),
        in_specs=[hbm, hbm, hbm, hbm, hbm, vmem, smem],
        out_specs=(vmem, vmem, vmem),
        scratch_shapes=[
            pltpu.VMEM((16, CHUNK, WIDTH), BF16),
            pltpu.VMEM((2, 8, 2, ROWS, WIDTH), BF16),
            pltpu.VMEM((ROWS, WIDTH), BF16),
            pltpu.VMEM((16 * ROWS, WIDTH), F32),
            pltpu.VMEM((16 * ROWS, WIDTH), F32),
            pltpu.VMEM((16 * ROWS, WIDTH), F32),
            pltpu.VMEM((32, 16 * ROWS), F32),
            pltpu.VMEM((8, 16 * ROWS), F32),
            pltpu.VMEM((32, 128), jnp.int32),
            pltpu.VMEM((16, ROWS, WIDTH), BF16),
            pltpu.VMEM((16, ROWS, WIDTH), BF16),
            pltpu.VMEM((8, 2, ROWS, WIDTH), BF16),
            pltpu.VMEM((8, 2, ROWS, WIDTH), BF16),
            pltpu.VMEM((8, 2, ROWS, WIDTH), BF16),
            pltpu.VMEM((8, 2, ROWS, WIDTH), BF16),
            pltpu.VMEM((2, ROWS, WIDTH), BF16),
            dma((5,)), dma((16,)), dma((16,)), dma((8,)), dma((8,)), dma((8,)), dma((8,)),
            dma((16,)), dma((16,)), dma((8,)), dma((8,)), dma((8,)), dma((8,)), dma, dma,
        ],
        compiler_params=pltpu.CompilerParams(
            collective_id=0, has_side_effects=True, vmem_limit_bytes=48 << 20
        ),
    )(
        queries, keys_in, values_in, outputs_saved, out_grad,
        log_sum.reshape(1, ROWS), block_table,
    )


def solution(mesh):
    rows = P(("pb", "ka"), None)
    return jax.shard_map(
        per_device,
        mesh=mesh,
        in_specs=(rows, rows, rows, rows, rows, P(("pb", "ka")), P()),
        out_specs=(rows, rows, rows),
        check_vma=False,
    )
```

```python
import math

import jax
import jax.numpy as jnp
from jax import lax
from jax.experimental import pallas as pl
from jax.experimental.pallas import tpu as pltpu
from jax.sharding import PartitionSpec as P

MESH = pl.DeviceIdType.MESH
F32, BF16 = jnp.float32, jnp.bfloat16
ROWS = 160
BLK = 80
WIDTH = 128
SCALE = 1.0 / math.sqrt(WIDTH)
TO_EXP2 = SCALE * math.log2(math.e)
LOG2E = math.log2(math.e)
HIDDEN = 1e30
CHUNK = 336
PLANE = (
    (0, 0), (1, 0), (3, 0), (0, 1), (0, 3), (2, 0), (0, 2), (1, 1),
    (2, 2), (2, 1), (2, 3), (1, 2), (3, 2), (3, 3), (1, 3), (3, 1),
)
LINE = (0, 1, -1, 2, -2, 3, -3, 4)
Q_TILE, K_TILE = 4 * ROWS, 4 * ROWS
NT = (((1,), (1,)), ((), ()))
TN = (((0,), (0,)), ((), ()))


def place():
    pb, ka = lax.axis_index("pb"), lax.axis_index("ka")
    x, y, z, c = (ka // 2) % 4, ka // 8, (pb // 2) * 2 + ka % 2, pb % 2
    return x, y, z, c


def device(x, y, z, c):
    return ((z // 2) * 2 + c, y * 8 + x * 2 + z % 2)


def storage(x, y, z, c):
    pb, ka = device(x, y, z, c)
    return pb * 32 + ka


def kernel(
    q_in, k_in, v_in, o_in, g_in, l_in, table,
    dq_out, dk_out, dv_out,
    qg, kv, o_own, dq_acc, dk_acc, dv_acc, lrow, drow, keyid,
    dq_send, dq_recv, sib_send, sib_recv, dkv_send, dkv_recv, relay_recv, dkv_cross,
    local_sem, q_ss, q_rs, kz_ss, kz_rs, kc_ss, kc_rs,
    dq_ss, dq_rs, sib_ss, sib_rs, dkv_ss, dkv_rs, cross_ss, cross_rs,
):
    x, y, z, c = place()
    other = 1 - c

    def plane_dev(i, sign):
        dx, dy = PLANE[i]
        return device((x + sign * dx + 4) % 4, (y + sign * dy + 4) % 4, z, c)

    def line_dev(dz, core):
        return device(x, y, (z + dz + 8) % 8, core)

    sibling = device(x, y, z, other)
    partners = [plane_dev(i, 1) for i in range(1, 16)]
    partners += [line_dev(dz, c) for dz in (1, -1, 2, -2)]
    partners += [sibling, line_dev(1, other), line_dev(-1, other)]
    barrier = pltpu.get_barrier_semaphore()
    for p in partners:
        pl.semaphore_signal(barrier, inc=1, device_id=p, device_id_type=MESH)

    loads = [
        pltpu.make_async_copy(g_in, qg.at[0, pl.ds(ROWS, ROWS)], local_sem.at[0]),
        pltpu.make_async_copy(o_in, o_own, local_sem.at[1]),
        pltpu.make_async_copy(q_in, qg.at[0, pl.ds(0, ROWS)], local_sem.at[2]),
        pltpu.make_async_copy(k_in, kv.at[0, 0, 0], local_sem.at[3]),
        pltpu.make_async_copy(v_in, kv.at[1, 0, 0], local_sem.at[4]),
    ]
    for cp in loads:
        cp.start()
    dq_acc[...] = jnp.zeros_like(dq_acc)
    dk_acc[...] = jnp.zeros_like(dk_acc)
    dv_acc[...] = jnp.zeros_like(dv_acc)
    for cp in loads:
        cp.wait()

    q0, g0 = qg[0, 0:ROWS, :], qg[0, ROWS : 2 * ROWS, :]
    k0, v0 = kv[0, 0, 0], kv[1, 0, 0]
    prod = g0.astype(F32) * o_own[...].astype(F32)
    high = prod.astype(BF16)
    low = (prod - high.astype(F32)).astype(BF16)
    ones = jnp.ones((8, WIDTH), BF16)
    delta8 = lax.dot_general(ones, high, NT, preferred_element_type=F32)
    delta8 += lax.dot_general(ones, low, NT, preferred_element_type=F32)
    delta = delta8[0:1, :]
    lse = l_in[...] * LOG2E
    sub = lax.broadcasted_iota(jnp.int32, (8, ROWS), 0)
    both = jnp.where(sub % 2 == 0, lse, delta)
    p1 = both.astype(BF16).astype(F32)
    p2 = (both - p1).astype(BF16).astype(F32)
    p3 = both - p1 - p2
    pieces = jnp.where(sub < 2, p1, jnp.where(sub < 4, p2, jnp.where(sub < 6, p3, 0.0)))
    wide = jnp.concatenate([pieces, jnp.zeros((8, 256 - ROWS), F32)], axis=1)
    first, rest = wide[:, 0:128], wide[:, 128:256]
    lane = lax.broadcasted_iota(jnp.int32, (8, 128), 1)
    second = jnp.where(
        lane < 48, pltpu.roll(first, 48, 1), pltpu.roll(rest, 48, 1)
    )
    keep = lane < BLK
    stats = jnp.concatenate(
        [jnp.where(keep, first, 0.0), jnp.where(keep, second, 0.0)], axis=0
    )
    qg[0, 2 * ROWS : CHUNK, :] = stats.astype(BF16)

    q_cps = {
        i: pltpu.make_async_remote_copy(
            src_ref=qg.at[0], dst_ref=qg.at[i],
            send_sem=q_ss.at[i], recv_sem=q_rs.at[i],
            device_id=plane_dev(i, -1), device_id_type=MESH,
        )
        for i in range(1, 16)
    }
    kz_cps = {}
    for s in range(1, 7):
        held, to = (0, -LINE[s]) if s < 5 else (s - 2, -1 if s == 5 else 1)
        kz_cps[s] = pltpu.make_async_remote_copy(
            src_ref=kv.at[:, held, 0], dst_ref=kv.at[:, s, 0],
            send_sem=kz_ss.at[s], recv_sem=kz_rs.at[s],
            device_id=line_dev(to, c), device_id_type=MESH,
        )
    for s, (part, held, to) in {7: (0, 3, -2), 8: (1, 4, 2)}.items():
        kz_cps[s] = pltpu.make_async_remote_copy(
            src_ref=kv.at[part, held, 0], dst_ref=kv.at[part, 7, 0],
            send_sem=kz_ss.at[s], recv_sem=kz_rs.at[s],
            device_id=line_dev(to, c), device_id_type=MESH,
        )
    kc_cps = [
        pltpu.make_async_remote_copy(
            src_ref=kv.at[:, s, 0], dst_ref=kv.at[:, s, 1],
            send_sem=kc_ss.at[s], recv_sem=kc_rs.at[s],
            device_id=sibling, device_id_type=MESH,
        )
        for s in range(8)
    ]

    pl.semaphore_wait(barrier, len(partners))
    for cp in (
        kz_cps[1], kz_cps[2], q_cps[1], q_cps[2], q_cps[3], q_cps[4], kc_cps[0],
        kz_cps[3], kz_cps[4], q_cps[5], q_cps[6], q_cps[7],
    ):
        cp.start()

    row = lax.broadcasted_iota(jnp.int32, (ROWS, ROWS), 0)
    col = lax.broadcasted_iota(jnp.int32, (ROWS, ROWS), 1)
    seen = (row <= col) & ((row >= BLK) == (col >= BLK))
    s0 = lax.dot_general(k0, q0, NT, preferred_element_type=F32)
    e0 = jnp.exp2(jnp.where(seen, s0 * TO_EXP2 - lse, -HIDDEN))
    dp0 = lax.dot_general(v0, g0, NT, preferred_element_type=F32)
    ds0 = (e0 * (dp0 - delta)).astype(BF16)
    dq_acc[0:ROWS, :] = lax.dot_general(ds0, k0, TN, preferred_element_type=F32)
    dk_acc[0:ROWS, :] = jnp.dot(ds0, q0, preferred_element_type=F32)
    dv_acc[0:ROWS, :] = jnp.dot(e0.astype(BF16), g0, preferred_element_type=F32)

    for r in range(32):
        s, h, b = r // 4, (r % 4) // 2, r % 2
        at = storage(x, y, (z + LINE[s] + 8) % 8, c if h == 0 else other) * 2 + b
        keyid[r : r + 1, :] = jnp.full((1, 128), table[at], jnp.int32)

    def rows_of(t):
        blocks = []
        for i in range(4 * t, 4 * t + 4):
            st = qg[i, 2 * ROWS : CHUNK, :].astype(F32)
            dx, dy = PLANE[i]
            at = storage((x + dx) % 4, (y + dy) % 4, z, c) * 2
            blocks += [(st[0:8, :], table[at]), (st[8:16, :], table[at + 1])]
        for j in range(5):
            acc = jnp.zeros((8, 128), F32)
            ids = jnp.zeros((8, 128), jnp.int32)
            for r, (st, entry) in enumerate(blocks):
                shift = BLK * r - 128 * j
                if shift <= -BLK or shift >= 128:
                    continue
                here = (lane >= max(shift, 0)) & (lane < min(128, shift + BLK))
                moved = st if shift % 128 == 0 else pltpu.roll(st, shift % 128, 1)
                acc = jnp.where(here, moved, acc)
                ids = jnp.where(here, entry, ids)
            lr = acc[0:1, :] + acc[2:3, :] + acc[4:5, :]
            dr = acc[1:2, :] + acc[3:4, :] + acc[5:6, :]
            cols = slice(Q_TILE * t + 128 * j, Q_TILE * t + 128 * (j + 1))
            drow[:, cols] = jnp.broadcast_to(dr, (8, 128))
            lb = jnp.broadcast_to(lr, (8, 128))
            for u in range(4):
                lrow[8 * u : 8 * u + 8, cols] = jnp.where(
                    ids > keyid[8 * u : 8 * u + 8, :], lb, HIDDEN
                )

    def tile(qi, ki):
        qs = pl.ds(pl.multiple_of(qi * Q_TILE, Q_TILE), Q_TILE)
        ks = pl.ds(pl.multiple_of(ki * K_TILE, K_TILE), K_TILE)
        q = qg[pl.ds(qi * 4, 4), 0:ROWS, :].reshape(Q_TILE, WIDTH)
        g = qg[pl.ds(qi * 4, 4), ROWS : 2 * ROWS, :].reshape(Q_TILE, WIDTH)
        k = kv[0, pl.ds(ki * 2, 2), :, :, :].reshape(K_TILE, WIDTH)
        v = kv[1, pl.ds(ki * 2, 2), :, :, :].reshape(K_TILE, WIDTH)
        s = lax.dot_general(k, q, NT, preferred_element_type=F32)
        dp = lax.dot_general(v, g, NT, preferred_element_type=F32)
        lr = lrow[pl.ds(pl.multiple_of(ki * 8, 8), 8), qs]
        bias = jnp.broadcast_to(lr[:, None, :], (8, BLK, Q_TILE)).reshape(K_TILE, Q_TILE)
        p = jnp.exp2(s * TO_EXP2 - bias)
        ds = (p * (dp - drow[0:1, qs])).astype(BF16)
        dv_acc[ks, :] += jnp.dot(p.astype(BF16), g, preferred_element_type=F32)
        dk_acc[ks, :] += jnp.dot(ds, q, preferred_element_type=F32)
        dq_acc[qs, :] += lax.dot_general(ds, k, TN, preferred_element_type=F32)

    dq_cps = {
        i: pltpu.make_async_remote_copy(
            src_ref=dq_send.at[i], dst_ref=dq_recv.at[i],
            send_sem=dq_ss.at[i], recv_sem=dq_rs.at[i],
            device_id=plane_dev(i, 1), device_id_type=MESH,
        )
        for i in range(1, 16)
    }
    sib_cps = {
        s: pltpu.make_async_remote_copy(
            src_ref=sib_send.at[s], dst_ref=sib_recv.at[s],
            send_sem=sib_ss.at[s], recv_sem=sib_rs.at[s],
            device_id=sibling, device_id_type=MESH,
        )
        for s in (0, 2, 3, 4, 5, 6, 7)
    }
    dkv_cps = {
        s: pltpu.make_async_remote_copy(
            src_ref=dkv_send.at[s], dst_ref=dkv_recv.at[s] if s < 5 else relay_recv.at[s - 5],
            send_sem=dkv_ss.at[s], recv_sem=dkv_rs.at[s],
            device_id=line_dev(LINE[s] if s < 5 else (1 if s == 5 else -1), c),
            device_id_type=MESH,
        )
        for s in range(1, 7)
    }
    for s, (part, to) in {7: (0, 2), 8: (1, -2)}.items():
        dkv_cps[s] = pltpu.make_async_remote_copy(
            src_ref=dkv_send.at[7, part], dst_ref=relay_recv.at[2, part],
            send_sem=dkv_ss.at[s], recv_sem=dkv_rs.at[s],
            device_id=line_dev(to, c), device_id_type=MESH,
        )
    cross = pltpu.make_async_remote_copy(
        src_ref=sib_send.at[1], dst_ref=dkv_cross,
        send_sem=cross_ss, recv_sem=cross_rs,
        device_id=line_dev(1, other), device_id_type=MESH,
    )

    def queries_out(t):
        for i in range(4 * t, 4 * t + 4):
            if i > 0:
                dq_send[i] = dq_acc[i * ROWS : (i + 1) * ROWS, :].astype(BF16)
                dq_cps[i].start()

    def part(acc, s, h):
        at = s * 2 * ROWS + h * ROWS
        return acc[at : at + ROWS, :]

    def to_sibling(s):
        sib_send[s, 0] = part(dk_acc, s, 1).astype(BF16)
        sib_send[s, 1] = part(dv_acc, s, 1).astype(BF16)
        (cross if s == 1 else sib_cps[s]).start()

    def to_owner(s):
        a, b = part(dk_acc, s, 0), part(dv_acc, s, 0)
        if s != 1:
            sib_cps[s].wait_recv()
            a = a + sib_recv[s, 0].astype(F32)
            b = b + sib_recv[s, 1].astype(F32)
        if s in (3, 4):
            dkv_cps[s + 2].wait_recv()
            dkv_cps[s + 4].wait_recv()
            a = a + relay_recv[s - 3, 0].astype(F32)
            b = b + relay_recv[s - 3, 1].astype(F32)
            if s == 3:
                a = a + relay_recv[2, 0].astype(F32)
            else:
                b = b + relay_recv[2, 1].astype(F32)
        dkv_send[s, 0] = a.astype(BF16)
        dkv_send[s, 1] = b.astype(BF16)
        dkv_cps[s].start()
        if s == 7:
            dkv_cps[8].start()

    def before(n):
        if n == 0:
            for s in (1, 2):
                kz_cps[s].wait_recv()
                kc_cps[s].start()
            for i in (1, 2, 3, 4):
                q_cps[i].wait_recv()
            for i in range(15, 7, -1):
                q_cps[i].start()
            rows_of(0)
            kc_cps[0].wait_recv()
            kc_cps[1].wait_recv()
        if n == 1:
            for s in (3, 4):
                kz_cps[s].wait_recv()
                kz_cps[s + 2].start()
                kz_cps[s + 4].start()
                kc_cps[s].start()
            for i in (5, 6, 7):
                q_cps[i].wait_recv()
            rows_of(1)
        if n == 2:
            kc_cps[2].wait_recv()
            kc_cps[3].wait_recv()
        if n == 4:
            for s in (5, 6):
                kz_cps[s].wait_recv()
                kc_cps[s].start()
            kc_cps[4].wait_recv()
            kc_cps[5].wait_recv()
        if n == 6:
            kz_cps[7].wait_recv()
            kz_cps[8].wait_recv()
            kc_cps[7].start()
            kc_cps[6].wait_recv()
            kc_cps[7].wait_recv()
        if n == 8:
            queries_out(0)
            queries_out(1)
            for i in (8, 9, 10, 11):
                q_cps[i].wait_recv()
            rows_of(2)
        if n == 9:
            for i in (12, 13, 14, 15):
                q_cps[i].wait_recv()
            rows_of(3)
        if n == 10:
            to_sibling(6)
            to_sibling(7)
        if n == 11:
            to_owner(6)
            to_owner(7)
        if n == 12:
            to_sibling(5)
            to_sibling(4)
        if n == 13:
            to_owner(5)
        if n == 14:
            queries_out(2)
        if n == 15:
            to_sibling(3)
            to_sibling(2)

    def step(n, carry):
        qi = jnp.where(n < 8, n % 2, jnp.where(n < 12, 2 + n % 2, 2 + (n - 12) // 2))
        ki = jnp.where(n < 8, n // 2, jnp.where(n < 12, 3 - (n - 8) // 2, 1 - n % 2))
        for hook in (0, 1, 2, 4, 6, 8, 9, 10, 11, 12, 13, 14, 15):
            pl.when(n == hook)(lambda hook=hook: before(hook))
        tile(qi, ki)
        return carry

    lax.fori_loop(0, 16, step, 0)

    to_sibling(1)
    to_owner(1)
    to_sibling(0)
    queries_out(3)
    for s in (4, 2, 3):
        to_owner(s)

    a, b = part(dk_acc, 0, 0), part(dv_acc, 0, 0)
    sib_cps[0].wait_recv()
    a, b = a + sib_recv[0, 0].astype(F32), b + sib_recv[0, 1].astype(F32)
    total = dq_acc[0:ROWS, :]
    for i in range(1, 16):
        dq_cps[i].wait_recv()
        total = total + dq_recv[i].astype(F32)
    dq_out[...] = (total * SCALE).astype(BF16)
    cross.wait_recv()
    a, b = a + dkv_cross[0].astype(F32), b + dkv_cross[1].astype(F32)
    for s in range(1, 5):
        dkv_cps[s].wait_recv()
        a, b = a + dkv_recv[s, 0].astype(F32), b + dkv_recv[s, 1].astype(F32)
    dk_out[...] = (a * SCALE).astype(BF16)
    dv_out[...] = b.astype(BF16)

    for group in (q_cps, kz_cps, dq_cps, dkv_cps, sib_cps):
        for cp in group.values():
            cp.wait_send()
    for cp in kc_cps:
        cp.wait_send()
    cross.wait_send()


def per_device(queries, keys_in, values_in, outputs_saved, out_grad, log_sum, block_table):
    hbm = pl.BlockSpec(memory_space=pl.ANY)
    vmem = pl.BlockSpec(memory_space=pltpu.VMEM)
    smem = pl.BlockSpec(memory_space=pltpu.SMEM)
    dma = pltpu.SemaphoreType.DMA
    out = jax.ShapeDtypeStruct((ROWS, WIDTH), BF16)
    return pl.pallas_call(
        kernel,
        out_shape=(out, out, out),
        in_specs=[hbm, hbm, hbm, hbm, hbm, vmem, smem],
        out_specs=(vmem, vmem, vmem),
        scratch_shapes=[
            pltpu.VMEM((16, CHUNK, WIDTH), BF16),
            pltpu.VMEM((2, 8, 2, ROWS, WIDTH), BF16),
            pltpu.VMEM((ROWS, WIDTH), BF16),
            pltpu.VMEM((16 * ROWS, WIDTH), F32),
            pltpu.VMEM((16 * ROWS, WIDTH), F32),
            pltpu.VMEM((16 * ROWS, WIDTH), F32),
            pltpu.VMEM((32, 16 * ROWS), F32),
            pltpu.VMEM((8, 16 * ROWS), F32),
            pltpu.VMEM((32, 128), jnp.int32),
            pltpu.VMEM((16, ROWS, WIDTH), BF16),
            pltpu.VMEM((16, ROWS, WIDTH), BF16),
            pltpu.VMEM((8, 2, ROWS, WIDTH), BF16),
            pltpu.VMEM((8, 2, ROWS, WIDTH), BF16),
            pltpu.VMEM((8, 2, ROWS, WIDTH), BF16),
            pltpu.VMEM((5, 2, ROWS, WIDTH), BF16),
            pltpu.VMEM((3, 2, ROWS, WIDTH), BF16),
            pltpu.VMEM((2, ROWS, WIDTH), BF16),
            dma((5,)), dma((16,)), dma((16,)), dma((9,)), dma((9,)), dma((8,)), dma((8,)),
            dma((16,)), dma((16,)), dma((8,)), dma((8,)), dma((9,)), dma((9,)), dma, dma,
        ],
        compiler_params=pltpu.CompilerParams(
            collective_id=0, has_side_effects=True, vmem_limit_bytes=60 << 20
        ),
    )(
        queries, keys_in, values_in, outputs_saved, out_grad,
        log_sum.reshape(1, ROWS), block_table,
    )


def solution(mesh):
    rows = P(("pb", "ka"), None)
    return jax.shard_map(
        per_device,
        mesh=mesh,
        in_specs=(rows, rows, rows, rows, rows, P(("pb", "ka")), P()),
        out_specs=(rows, rows, rows),
        check_vma=False,
    )
```

```python
import math

import jax
import jax.numpy as jnp
from jax import lax
from jax.experimental import pallas as pl
from jax.experimental.pallas import tpu as pltpu
from jax.sharding import PartitionSpec as P

MESH = pl.DeviceIdType.MESH
F32, BF16 = jnp.float32, jnp.bfloat16
ROWS = 160
BLK = 80
WIDTH = 128
SCALE = 1.0 / math.sqrt(WIDTH)
TO_EXP2 = SCALE * math.log2(math.e)
LOG2E = math.log2(math.e)
HIDDEN = 1e30
CHUNK = 336
PLANE = (
    (0, 0), (1, 0), (3, 0), (0, 1), (0, 3), (2, 0), (0, 2), (1, 1),
    (2, 2), (2, 1), (2, 3), (1, 2), (3, 2), (3, 3), (1, 3), (3, 1),
)
LINE = (
    (0, 0), (1, 0), (-1, 0), (0, 1), (1, 1), (-1, 1), (2, 0), (-2, 0),
    (2, 1), (-2, 1), (3, 0), (-3, 0), (3, 1), (-3, 1), (4, 0), (4, 1),
)
MINE = {dz: LINE.index((dz, 0)) for dz in (0, 1, -1, 2, -2, 3, -3, 4)}
THEIRS = {dz: LINE.index((dz, 1)) for dz in (0, 1, -1, 2, -2, 3, -3, 4)}
TILES = (
    (0, 0), (0, 1), (1, 1), (1, 0), (1, 2), (0, 2), (0, 3), (1, 3),
    (2, 3), (3, 3), (3, 2), (2, 2), (2, 1), (2, 0), (3, 1), (3, 0),
)
Q_TILE, K_TILE = 4 * ROWS, 4 * ROWS
NT = (((1,), (1,)), ((), ()))
TN = (((0,), (0,)), ((), ()))


def pick(values, n):
    out = values[0]
    for i in range(1, len(values)):
        out = jnp.where(n == i, values[i], out)
    return out


def place():
    pb, ka = lax.axis_index("pb"), lax.axis_index("ka")
    x, y, z, c = (ka // 2) % 4, ka // 8, (pb // 2) * 2 + ka % 2, pb % 2
    return x, y, z, c


def device(x, y, z, c):
    return ((z // 2) * 2 + c, y * 8 + x * 2 + z % 2)


def storage(x, y, z, c):
    pb, ka = device(x, y, z, c)
    return pb * 32 + ka


def kernel(
    q_in, k_in, v_in, o_in, g_in, l_in, table,
    dq_out, dk_out, dv_out,
    qg, kv, o_own, dq_acc, dk_acc, dv_acc, lrow, drow, keyid,
    dq_send, dq_recv, sib_send, sib_recv, dkv_send, dkv_recv,
    local_sem, q_ss, q_rs, kz_ss, kz_rs, kc_ss, kc_rs,
    dq_ss, dq_rs, sib_ss, sib_rs, dkv_ss, dkv_rs,
):
    x, y, z, c = place()
    other = 1 - c

    def plane_dev(i, sign):
        dx, dy = PLANE[i]
        return device((x + sign * dx + 4) % 4, (y + sign * dy + 4) % 4, z, c)

    def line_dev(dz, core):
        return device(x, y, (z + dz + 8) % 8, core)

    sibling = device(x, y, z, other)
    partners = [plane_dev(i, 1) for i in range(1, 16)]
    partners += [line_dev(dz, c) for dz in (1, -1, 2, -2)] + [sibling]
    barrier = pltpu.get_barrier_semaphore()
    for p in partners:
        pl.semaphore_signal(barrier, inc=1, device_id=p, device_id_type=MESH)

    loads = [
        pltpu.make_async_copy(g_in, qg.at[0, pl.ds(ROWS, ROWS)], local_sem.at[0]),
        pltpu.make_async_copy(o_in, o_own, local_sem.at[1]),
        pltpu.make_async_copy(q_in, qg.at[0, pl.ds(0, ROWS)], local_sem.at[2]),
        pltpu.make_async_copy(k_in, kv.at[0, 0], local_sem.at[3]),
        pltpu.make_async_copy(v_in, kv.at[1, 0], local_sem.at[4]),
    ]
    for cp in loads:
        cp.start()
    dq_acc[...] = jnp.zeros_like(dq_acc)
    dk_acc[...] = jnp.zeros_like(dk_acc)
    dv_acc[...] = jnp.zeros_like(dv_acc)
    for cp in loads:
        cp.wait()

    q0, g0 = qg[0, 0:ROWS, :], qg[0, ROWS : 2 * ROWS, :]
    k0, v0 = kv[0, 0], kv[1, 0]
    prod = g0.astype(F32) * o_own[...].astype(F32)
    high = prod.astype(BF16)
    low = (prod - high.astype(F32)).astype(BF16)
    ones = jnp.ones((8, WIDTH), BF16)
    delta8 = lax.dot_general(ones, high, NT, preferred_element_type=F32)
    delta8 += lax.dot_general(ones, low, NT, preferred_element_type=F32)
    delta = delta8[0:1, :]
    lse = l_in[...] * LOG2E
    sub = lax.broadcasted_iota(jnp.int32, (8, ROWS), 0)
    both = jnp.where(sub % 2 == 0, lse, delta)
    p1 = both.astype(BF16).astype(F32)
    p2 = (both - p1).astype(BF16).astype(F32)
    p3 = both - p1 - p2
    pieces = jnp.where(sub < 2, p1, jnp.where(sub < 4, p2, jnp.where(sub < 6, p3, 0.0)))
    wide = jnp.concatenate([pieces, jnp.zeros((8, 256 - ROWS), F32)], axis=1)
    first, rest = wide[:, 0:128], wide[:, 128:256]
    lane = lax.broadcasted_iota(jnp.int32, (8, 128), 1)
    second = jnp.where(
        lane < 48, pltpu.roll(first, 48, 1), pltpu.roll(rest, 48, 1)
    )
    keep = lane < BLK
    stats = jnp.concatenate(
        [jnp.where(keep, first, 0.0), jnp.where(keep, second, 0.0)], axis=0
    )
    qg[0, 2 * ROWS : CHUNK, :] = stats.astype(BF16)

    def q_copy(i, held, dx, dy, sem, rows=(0, CHUNK)):
        return pltpu.make_async_remote_copy(
            src_ref=qg.at[held, pl.ds(*rows)], dst_ref=qg.at[i, pl.ds(*rows)],
            send_sem=q_ss.at[sem], recv_sem=q_rs.at[sem],
            device_id=device((x - dx + 4) % 4, (y - dy + 4) % 4, z, c), device_id_type=MESH,
        )

    at = {offset: i for i, offset in enumerate(PLANE)}
    q_cps = {}
    for offset in ((1, 0), (3, 0), (0, 1), (0, 3), (2, 0), (0, 2)):
        q_cps[at[offset]] = q_copy(at[offset], 0, *offset, at[offset])
    for dx, dy in ((1, 1), (3, 3), (1, 2), (3, 2)):
        q_cps[at[dx, dy]] = q_copy(at[dx, dy], at[0, dy], dx, 0, at[dx, dy])
    for dx, dy in ((1, 3), (3, 1), (2, 1), (2, 3)):
        q_cps[at[dx, dy]] = q_copy(at[dx, dy], at[dx, 0], 0, dy, at[dx, dy])
    far = at[2, 2]
    q_cps[far] = q_copy(far, at[0, 2], 2, 0, far, (0, 176))
    q_cps[16] = q_copy(far, at[2, 0], 0, 2, 16, (176, CHUNK - 176))

    kz_cps = {}
    for dz, (held, step) in {
        1: (0, 1), -1: (0, -1), 2: (0, 2), -2: (0, -2), 3: (1, 2), -3: (-1, -2),
    }.items():
        kz_cps[dz] = pltpu.make_async_remote_copy(
            src_ref=kv.at[:, MINE[held]], dst_ref=kv.at[:, MINE[dz]],
            send_sem=kz_ss.at[dz + 3], recv_sem=kz_rs.at[dz + 3],
            device_id=line_dev(-step, c), device_id_type=MESH,
        )
    for name, part, step in ((4, 0, 2), (5, 1, -2)):
        kz_cps[name] = pltpu.make_async_remote_copy(
            src_ref=kv.at[part, MINE[step]], dst_ref=kv.at[part, MINE[4]],
            send_sem=kz_ss.at[name + 3], recv_sem=kz_rs.at[name + 3],
            device_id=line_dev(-step, c), device_id_type=MESH,
        )
    kc_cps = {
        dz: pltpu.make_async_remote_copy(
            src_ref=kv.at[:, MINE[dz]], dst_ref=kv.at[:, THEIRS[dz]],
            send_sem=kc_ss.at[dz + 3], recv_sem=kc_rs.at[dz + 3],
            device_id=sibling, device_id_type=MESH,
        )
        for dz in MINE
    }

    pl.semaphore_wait(barrier, len(partners))
    for cp in (
        kz_cps[1], kz_cps[-1], q_cps[at[1, 0]], q_cps[at[3, 0]], q_cps[at[0, 1]], q_cps[at[0, 3]],
        kc_cps[0], kz_cps[2], kz_cps[-2], q_cps[at[2, 0]], q_cps[at[0, 2]],
    ):
        cp.start()

    row = lax.broadcasted_iota(jnp.int32, (ROWS, ROWS), 0)
    col = lax.broadcasted_iota(jnp.int32, (ROWS, ROWS), 1)
    seen = (row <= col) & ((row >= BLK) == (col >= BLK))
    s0 = lax.dot_general(k0, q0, NT, preferred_element_type=F32)
    e0 = jnp.exp2(jnp.where(seen, s0 * TO_EXP2 - lse, -HIDDEN))
    dp0 = lax.dot_general(v0, g0, NT, preferred_element_type=F32)
    ds0 = (e0 * (dp0 - delta)).astype(BF16)
    dq_acc[0:ROWS, :] = lax.dot_general(ds0, k0, TN, preferred_element_type=F32)
    dk_acc[0:ROWS, :] = jnp.dot(ds0, q0, preferred_element_type=F32)
    dv_acc[0:ROWS, :] = jnp.dot(e0.astype(BF16), g0, preferred_element_type=F32)

    for r in range(32):
        dz, h = LINE[r // 2]
        entry = storage(x, y, (z + dz + 8) % 8, c if h == 0 else other) * 2 + r % 2
        keyid[r : r + 1, :] = jnp.full((1, 128), table[entry], jnp.int32)

    def rows_of(t):
        blocks = []
        for i in range(4 * t, 4 * t + 4):
            st = qg[i, 2 * ROWS : CHUNK, :].astype(F32)
            dx, dy = PLANE[i]
            entry = storage((x + dx) % 4, (y + dy) % 4, z, c) * 2
            blocks += [(st[0:8, :], table[entry]), (st[8:16, :], table[entry + 1])]
        for j in range(5):
            acc = jnp.zeros((8, 128), F32)
            ids = jnp.zeros((8, 128), jnp.int32)
            for r, (st, entry) in enumerate(blocks):
                shift = BLK * r - 128 * j
                if shift <= -BLK or shift >= 128:
                    continue
                here = (lane >= max(shift, 0)) & (lane < min(128, shift + BLK))
                moved = st if shift % 128 == 0 else pltpu.roll(st, shift % 128, 1)
                acc = jnp.where(here, moved, acc)
                ids = jnp.where(here, entry, ids)
            lr = acc[0:1, :] + acc[2:3, :] + acc[4:5, :]
            dr = acc[1:2, :] + acc[3:4, :] + acc[5:6, :]
            cols = slice(Q_TILE * t + 128 * j, Q_TILE * t + 128 * (j + 1))
            drow[:, cols] = jnp.broadcast_to(dr, (8, 128))
            lb = jnp.broadcast_to(lr, (8, 128))
            for u in range(4):
                lrow[8 * u : 8 * u + 8, cols] = jnp.where(
                    ids > keyid[8 * u : 8 * u + 8, :], lb, HIDDEN
                )

    def tile(qi, ki):
        qs = pl.ds(pl.multiple_of(qi * Q_TILE, Q_TILE), Q_TILE)
        ks = pl.ds(pl.multiple_of(ki * K_TILE, K_TILE), K_TILE)
        q = qg[pl.ds(qi * 4, 4), 0:ROWS, :].reshape(Q_TILE, WIDTH)
        g = qg[pl.ds(qi * 4, 4), ROWS : 2 * ROWS, :].reshape(Q_TILE, WIDTH)
        k = kv[0, pl.ds(ki * 4, 4), :, :].reshape(K_TILE, WIDTH)
        v = kv[1, pl.ds(ki * 4, 4), :, :].reshape(K_TILE, WIDTH)
        s = lax.dot_general(k, q, NT, preferred_element_type=F32)
        dp = lax.dot_general(v, g, NT, preferred_element_type=F32)
        lr = lrow[pl.ds(pl.multiple_of(ki * 8, 8), 8), qs]
        bias = jnp.broadcast_to(lr[:, None, :], (8, BLK, Q_TILE)).reshape(K_TILE, Q_TILE)
        p = jnp.exp2(s * TO_EXP2 - bias)
        ds = (p * (dp - drow[0:1, qs])).astype(BF16)
        dv_acc[ks, :] += jnp.dot(p.astype(BF16), g, preferred_element_type=F32)
        dk_acc[ks, :] += jnp.dot(ds, q, preferred_element_type=F32)
        dq_acc[qs, :] += lax.dot_general(ds, k, TN, preferred_element_type=F32)

    dq_cps = {
        i: pltpu.make_async_remote_copy(
            src_ref=dq_send.at[i], dst_ref=dq_recv.at[i],
            send_sem=dq_ss.at[i], recv_sem=dq_rs.at[i],
            device_id=plane_dev(i, 1), device_id_type=MESH,
        )
        for i in range(1, 16)
    }
    sib_cps = {
        dz: pltpu.make_async_remote_copy(
            src_ref=sib_send.at[dz + 3], dst_ref=sib_recv.at[dz + 3],
            send_sem=sib_ss.at[dz + 3], recv_sem=sib_rs.at[dz + 3],
            device_id=sibling, device_id_type=MESH,
        )
        for dz in MINE
    }
    dkv_cps = {
        dz: pltpu.make_async_remote_copy(
            src_ref=dkv_send.at[dz + 3], dst_ref=dkv_recv.at[dz + 3],
            send_sem=dkv_ss.at[dz + 3], recv_sem=dkv_rs.at[dz + 3],
            device_id=line_dev(step, c), device_id_type=MESH,
        )
        for dz, step in {1: 1, -1: -1, 2: 2, -2: -2, 3: 2, -3: -2}.items()
    }
    for name, part, step in ((4, 0, 2), (5, 1, -2)):
        dkv_cps[name] = pltpu.make_async_remote_copy(
            src_ref=dkv_send.at[7, part], dst_ref=dkv_recv.at[7, part],
            send_sem=dkv_ss.at[name + 3], recv_sem=dkv_rs.at[name + 3],
            device_id=line_dev(step, c), device_id_type=MESH,
        )

    def queries_out(t):
        for i in range(4 * t, 4 * t + 4):
            if i > 0:
                dq_send[i] = dq_acc[i * ROWS : (i + 1) * ROWS, :].astype(BF16)
                dq_cps[i].start()

    def part(acc, i):
        return acc[i * ROWS : (i + 1) * ROWS, :]

    def to_sibling(dz):
        sib_send[dz + 3, 0] = part(dk_acc, THEIRS[dz]).astype(BF16)
        sib_send[dz + 3, 1] = part(dv_acc, THEIRS[dz]).astype(BF16)
        sib_cps[dz].start()

    def chip_sum(dz):
        sib_cps[dz].wait_recv()
        a = part(dk_acc, MINE[dz]) + sib_recv[dz + 3, 0].astype(F32)
        b = part(dv_acc, MINE[dz]) + sib_recv[dz + 3, 1].astype(F32)
        return a, b

    def to_owner(dz):
        a, b = chip_sum(dz)
        if dz in (1, -1):
            dkv_cps[3 * dz].wait_recv()
            a = a + dkv_recv[3 * dz + 3, 0].astype(F32)
            b = b + dkv_recv[3 * dz + 3, 1].astype(F32)
        if dz == 2:
            dkv_cps[4].wait_recv()
            a = a + dkv_recv[7, 0].astype(F32)
        if dz == -2:
            dkv_cps[5].wait_recv()
            b = b + dkv_recv[7, 1].astype(F32)
        dkv_send[dz + 3, 0] = a.astype(BF16)
        dkv_send[dz + 3, 1] = b.astype(BF16)
        dkv_cps[dz].start()
        if dz == 4:
            dkv_cps[5].start()

    def before(n):
        if n == 0:
            for offset in ((1, 0), (3, 0), (0, 1), (0, 3)):
                q_cps[at[offset]].wait_recv()
            for offset in ((1, 1), (3, 3), (1, 3), (3, 1)):
                q_cps[at[offset]].start()
            for dz in (1, -1):
                kz_cps[dz].wait_recv()
                kz_cps[3 * dz].start()
                kc_cps[dz].start()
            rows_of(0)
            kc_cps[0].wait_recv()
        if n == 1:
            for dz in (2, -2):
                kz_cps[dz].wait_recv()
                kz_cps[4 if dz == 2 else 5].start()
                kc_cps[dz].start()
            for offset in ((2, 0), (0, 2)):
                q_cps[at[offset]].wait_recv()
            for i in (at[1, 2], at[2, 1], at[3, 2], at[2, 3], far, 16):
                q_cps[i].start()
            kc_cps[1].wait_recv()
            kc_cps[-1].wait_recv()
        if n == 2:
            q_cps[at[1, 1]].wait_recv()
            rows_of(1)
        if n == 4:
            for dz in (3, -3):
                kz_cps[dz].wait_recv()
                kc_cps[dz].start()
            kc_cps[2].wait_recv()
            kc_cps[-2].wait_recv()
        if n == 5:
            kz_cps[4].wait_recv()
            kz_cps[5].wait_recv()
            kc_cps[4].start()
        if n == 6:
            for dz in (3, -3, 4):
                kc_cps[dz].wait_recv()
        if n == 8:
            queries_out(0)
            queries_out(1)
            for i in (8, 9, 10, 11, 16):
                q_cps[i].wait_recv()
            rows_of(2)
        if n == 9:
            for i in (12, 13, 14, 15):
                q_cps[i].wait_recv()
            rows_of(3)
        if n == 10:
            for dz in (4, 3, -3):
                to_sibling(dz)
        if n == 11:
            to_owner(4)
        if n == 12:
            to_owner(3)
            to_owner(-3)
            to_sibling(2)
            to_sibling(-2)
        if n == 14:
            queries_out(2)
        if n == 15:
            to_sibling(1)
            to_sibling(-1)
            to_owner(2)
            to_owner(-2)

    hooks = (0, 1, 2, 4, 5, 6, 8, 9, 10, 11, 12, 14, 15)

    def step(n, carry):
        for hook in hooks:
            pl.when(n == hook)(lambda hook=hook: before(hook))
        tile(pick([q for q, _ in TILES], n), pick([k for _, k in TILES], n))
        return carry

    lax.fori_loop(0, len(TILES), step, 0)

    to_sibling(0)
    to_owner(1)
    to_owner(-1)
    queries_out(3)

    a, b = chip_sum(0)
    total = dq_acc[0:ROWS, :]
    for i in range(1, 16):
        dq_cps[i].wait_recv()
        total = total + dq_recv[i].astype(F32)
    dq_out[...] = (total * SCALE).astype(BF16)
    for dz in (2, -2, 1, -1):
        dkv_cps[dz].wait_recv()
        a = a + dkv_recv[dz + 3, 0].astype(F32)
        b = b + dkv_recv[dz + 3, 1].astype(F32)
    dk_out[...] = (a * SCALE).astype(BF16)
    dv_out[...] = b.astype(BF16)

    for group in (q_cps, kz_cps, kc_cps, dq_cps, dkv_cps, sib_cps):
        for cp in group.values():
            cp.wait_send()


def per_device(queries, keys_in, values_in, outputs_saved, out_grad, log_sum, block_table):
    hbm = pl.BlockSpec(memory_space=pl.ANY)
    vmem = pl.BlockSpec(memory_space=pltpu.VMEM)
    smem = pl.BlockSpec(memory_space=pltpu.SMEM)
    dma = pltpu.SemaphoreType.DMA
    out = jax.ShapeDtypeStruct((ROWS, WIDTH), BF16)
    return pl.pallas_call(
        kernel,
        out_shape=(out, out, out),
        in_specs=[hbm, hbm, hbm, hbm, hbm, vmem, smem],
        out_specs=(vmem, vmem, vmem),
        scratch_shapes=[
            pltpu.VMEM((16, CHUNK, WIDTH), BF16),
            pltpu.VMEM((2, 16, ROWS, WIDTH), BF16),
            pltpu.VMEM((ROWS, WIDTH), BF16),
            pltpu.VMEM((16 * ROWS, WIDTH), F32),
            pltpu.VMEM((16 * ROWS, WIDTH), F32),
            pltpu.VMEM((16 * ROWS, WIDTH), F32),
            pltpu.VMEM((32, 16 * ROWS), F32),
            pltpu.VMEM((8, 16 * ROWS), F32),
            pltpu.VMEM((32, 128), jnp.int32),
            pltpu.VMEM((16, ROWS, WIDTH), BF16),
            pltpu.VMEM((16, ROWS, WIDTH), BF16),
            pltpu.VMEM((8, 2, ROWS, WIDTH), BF16),
            pltpu.VMEM((8, 2, ROWS, WIDTH), BF16),
            pltpu.VMEM((8, 2, ROWS, WIDTH), BF16),
            pltpu.VMEM((8, 2, ROWS, WIDTH), BF16),
            dma((5,)), dma((17,)), dma((17,)), dma((9,)), dma((9,)), dma((8,)), dma((8,)),
            dma((16,)), dma((16,)), dma((8,)), dma((8,)), dma((9,)), dma((9,)),
        ],
        compiler_params=pltpu.CompilerParams(
            collective_id=0, has_side_effects=True, vmem_limit_bytes=60 << 20
        ),
    )(
        queries, keys_in, values_in, outputs_saved, out_grad,
        log_sum.reshape(1, ROWS), block_table,
    )


def solution(mesh):
    rows = P(("pb", "ka"), None)
    return jax.shard_map(
        per_device,
        mesh=mesh,
        in_specs=(rows, rows, rows, rows, rows, P(("pb", "ka")), P()),
        out_specs=(rows, rows, rows),
        check_vma=False,
    )
```

```python
import math

import jax
import jax.numpy as jnp
from jax import lax
from jax.experimental import pallas as pl
from jax.experimental.pallas import tpu as pltpu
from jax.sharding import PartitionSpec as P

MESH = pl.DeviceIdType.MESH
F32, BF16 = jnp.float32, jnp.bfloat16
ROWS = 160
BLK = 80
WIDTH = 128
SCALE = 1.0 / math.sqrt(WIDTH)
TO_EXP2 = SCALE * math.log2(math.e)
LOG2E = math.log2(math.e)
HIDDEN = 1e30
CHUNK = 336
PLANE = (
    (0, 0), (1, 0), (3, 0), (0, 1), (0, 3), (2, 0), (0, 2), (1, 1),
    (2, 2), (2, 1), (2, 3), (1, 2), (3, 2), (3, 3), (1, 3), (3, 1),
)
LINE = (
    (0, 0), (1, 0), (-1, 0), (0, 1), (1, 1), (-1, 1), (2, 0), (-2, 0),
    (2, 1), (-2, 1), (3, 0), (-3, 0), (3, 1), (-3, 1), (4, 0), (4, 1),
)
MINE = {dz: LINE.index((dz, 0)) for dz in (0, 1, -1, 2, -2, 3, -3, 4)}
THEIRS = {dz: LINE.index((dz, 1)) for dz in (0, 1, -1, 2, -2, 3, -3, 4)}
TILES = (
    (0, 0), (0, 1), (1, 1), (1, 0), (1, 2), (0, 2), (0, 3), (1, 3),
    (2, 3), (3, 3), (3, 2), (2, 2), (2, 1), (2, 0), (3, 1), (3, 0),
)
Q_TILE, K_TILE = 4 * ROWS, 4 * ROWS
NT = (((1,), (1,)), ((), ()))
TN = (((0,), (0,)), ((), ()))


def pick(values, n):
    out = values[0]
    for i in range(1, len(values)):
        out = jnp.where(n == i, values[i], out)
    return out


def place():
    pb, ka = lax.axis_index("pb"), lax.axis_index("ka")
    x, y, z, c = (ka // 2) % 4, ka // 8, (pb // 2) * 2 + ka % 2, pb % 2
    return x, y, z, c


def device(x, y, z, c):
    return ((z // 2) * 2 + c, y * 8 + x * 2 + z % 2)


def storage(x, y, z, c):
    pb, ka = device(x, y, z, c)
    return pb * 32 + ka


def kernel(
    q_in, k_in, v_in, o_in, g_in, l_in, table,
    out,
    qg, kv, o_own, dq_acc, dk_acc, dv_acc, lrow, drow, keyid,
    dq_send, dq_recv, sib_send, sib_recv, dkv_send, dkv_recv,
    local_sem, q_ss, q_rs, kz_ss, kz_rs, kc_ss, kc_rs,
    dq_ss, dq_rs, sib_ss, sib_rs, dkv_ss, dkv_rs,
):
    x, y, z, c = place()
    other = 1 - c

    def plane_dev(i, sign):
        dx, dy = PLANE[i]
        return device((x + sign * dx + 4) % 4, (y + sign * dy + 4) % 4, z, c)

    def line_dev(dz, core):
        return device(x, y, (z + dz + 8) % 8, core)

    sibling = device(x, y, z, other)
    partners = [plane_dev(i, 1) for i in range(1, 16)]
    partners += [line_dev(dz, c) for dz in (1, -1, 2, -2)] + [sibling]
    barrier = pltpu.get_barrier_semaphore()
    for p in partners:
        pl.semaphore_signal(barrier, inc=1, device_id=p, device_id_type=MESH)

    loads = [
        pltpu.make_async_copy(k_in, kv.at[0, 0], local_sem.at[0]),
        pltpu.make_async_copy(v_in, kv.at[1, 0], local_sem.at[1]),
        pltpu.make_async_copy(g_in, qg.at[0, pl.ds(ROWS, ROWS)], local_sem.at[2]),
        pltpu.make_async_copy(o_in, o_own, local_sem.at[3]),
        pltpu.make_async_copy(q_in, qg.at[0, pl.ds(0, ROWS)], local_sem.at[4]),
    ]
    for cp in loads:
        cp.start()

    def q_copy(i, held, dx, dy, sem, rows=(0, CHUNK)):
        return pltpu.make_async_remote_copy(
            src_ref=qg.at[held, pl.ds(*rows)], dst_ref=qg.at[i, pl.ds(*rows)],
            send_sem=q_ss.at[sem], recv_sem=q_rs.at[sem],
            device_id=device((x - dx + 4) % 4, (y - dy + 4) % 4, z, c), device_id_type=MESH,
        )

    at = {offset: i for i, offset in enumerate(PLANE)}
    q_cps = {}
    for offset in ((1, 0), (3, 0), (0, 1), (0, 3), (2, 0), (0, 2)):
        q_cps[at[offset]] = q_copy(at[offset], 0, *offset, at[offset])
    for dx, dy in ((1, 1), (3, 3), (1, 2), (3, 2)):
        q_cps[at[dx, dy]] = q_copy(at[dx, dy], at[0, dy], dx, 0, at[dx, dy])
    for dx, dy in ((1, 3), (3, 1), (2, 1), (2, 3)):
        q_cps[at[dx, dy]] = q_copy(at[dx, dy], at[dx, 0], 0, dy, at[dx, dy])
    far = at[2, 2]
    q_cps[far] = q_copy(far, at[0, 2], 2, 0, far, (0, 176))
    q_cps[16] = q_copy(far, at[2, 0], 0, 2, 16, (176, CHUNK - 176))

    kz_cps = {}
    for dz, (held, step) in {
        1: (0, 1), -1: (0, -1), 2: (0, 2), -2: (0, -2), 3: (1, 2), -3: (-1, -2),
    }.items():
        kz_cps[dz] = pltpu.make_async_remote_copy(
            src_ref=kv.at[:, MINE[held]], dst_ref=kv.at[:, MINE[dz]],
            send_sem=kz_ss.at[dz + 3], recv_sem=kz_rs.at[dz + 3],
            device_id=line_dev(-step, c), device_id_type=MESH,
        )
    for name, part, step in ((4, 0, 2), (5, 1, -2)):
        kz_cps[name] = pltpu.make_async_remote_copy(
            src_ref=kv.at[part, MINE[step]], dst_ref=kv.at[part, MINE[4]],
            send_sem=kz_ss.at[name + 3], recv_sem=kz_rs.at[name + 3],
            device_id=line_dev(-step, c), device_id_type=MESH,
        )
    kc_cps = {
        dz: pltpu.make_async_remote_copy(
            src_ref=kv.at[:, MINE[dz]], dst_ref=kv.at[:, THEIRS[dz]],
            send_sem=kc_ss.at[dz + 3], recv_sem=kc_rs.at[dz + 3],
            device_id=sibling, device_id_type=MESH,
        )
        for dz in MINE
    }

    for cp in loads[:2]:
        cp.wait()
    pl.semaphore_wait(barrier, len(partners))
    for dz in (1, -1):
        kz_cps[dz].start()
    kc_cps[0].start()
    for dz in (2, -2):
        kz_cps[dz].start()

    for cp in loads[2:]:
        cp.wait()
    q0, g0 = qg[0, 0:ROWS, :], qg[0, ROWS : 2 * ROWS, :]
    k0, v0 = kv[0, 0], kv[1, 0]
    prod = g0.astype(F32) * o_own[...].astype(F32)
    high = prod.astype(BF16)
    low = (prod - high.astype(F32)).astype(BF16)
    ones = jnp.ones((8, WIDTH), BF16)
    delta8 = lax.dot_general(ones, high, NT, preferred_element_type=F32)
    delta8 += lax.dot_general(ones, low, NT, preferred_element_type=F32)
    delta = delta8[0:1, :]
    lse = l_in[...] * LOG2E
    sub = lax.broadcasted_iota(jnp.int32, (8, ROWS), 0)
    both = jnp.where(sub % 2 == 0, lse, delta)
    p1 = both.astype(BF16).astype(F32)
    p2 = (both - p1).astype(BF16).astype(F32)
    p3 = both - p1 - p2
    pieces = jnp.where(sub < 2, p1, jnp.where(sub < 4, p2, jnp.where(sub < 6, p3, 0.0)))
    wide = jnp.concatenate([pieces, jnp.zeros((8, 256 - ROWS), F32)], axis=1)
    first, rest = wide[:, 0:128], wide[:, 128:256]
    lane = lax.broadcasted_iota(jnp.int32, (8, 128), 1)
    second = jnp.where(
        lane < 48, pltpu.roll(first, 48, 1), pltpu.roll(rest, 48, 1)
    )
    keep = lane < BLK
    stats = jnp.concatenate(
        [jnp.where(keep, first, 0.0), jnp.where(keep, second, 0.0)], axis=0
    )
    qg[0, 2 * ROWS : CHUNK, :] = stats.astype(BF16)

    for offset in ((1, 0), (3, 0), (0, 1), (0, 3), (2, 0), (0, 2)):
        q_cps[at[offset]].start()
    dq_acc[...] = jnp.zeros_like(dq_acc)
    dk_acc[...] = jnp.zeros_like(dk_acc)
    dv_acc[...] = jnp.zeros_like(dv_acc)

    row = lax.broadcasted_iota(jnp.int32, (ROWS, ROWS), 0)
    col = lax.broadcasted_iota(jnp.int32, (ROWS, ROWS), 1)
    seen = (row <= col) & ((row >= BLK) == (col >= BLK))
    s0 = lax.dot_general(k0, q0, NT, preferred_element_type=F32)
    e0 = jnp.exp2(jnp.where(seen, s0 * TO_EXP2 - lse, -HIDDEN))
    dp0 = lax.dot_general(v0, g0, NT, preferred_element_type=F32)
    ds0 = (e0 * (dp0 - delta)).astype(BF16)
    dq_acc[0:ROWS, :] = lax.dot_general(ds0, k0, TN, preferred_element_type=F32)
    dk_acc[0:ROWS, :] = jnp.dot(ds0, q0, preferred_element_type=F32)
    dv_acc[0:ROWS, :] = jnp.dot(e0.astype(BF16), g0, preferred_element_type=F32)

    for r in range(32):
        dz, h = LINE[r // 2]
        entry = storage(x, y, (z + dz + 8) % 8, c if h == 0 else other) * 2 + r % 2
        keyid[r : r + 1, :] = jnp.full((1, 128), table[entry], jnp.int32)

    def rows_of(t):
        blocks = []
        for i in range(4 * t, 4 * t + 4):
            st = qg[i, 2 * ROWS : CHUNK, :].astype(F32)
            dx, dy = PLANE[i]
            entry = storage((x + dx) % 4, (y + dy) % 4, z, c) * 2
            blocks += [(st[0:8, :], table[entry]), (st[8:16, :], table[entry + 1])]
        for j in range(5):
            acc = jnp.zeros((8, 128), F32)
            ids = jnp.zeros((8, 128), jnp.int32)
            for r, (st, entry) in enumerate(blocks):
                shift = BLK * r - 128 * j
                if shift <= -BLK or shift >= 128:
                    continue
                here = (lane >= max(shift, 0)) & (lane < min(128, shift + BLK))
                moved = st if shift % 128 == 0 else pltpu.roll(st, shift % 128, 1)
                acc = jnp.where(here, moved, acc)
                ids = jnp.where(here, entry, ids)
            lr = acc[0:1, :] + acc[2:3, :] + acc[4:5, :]
            dr = acc[1:2, :] + acc[3:4, :] + acc[5:6, :]
            cols = slice(Q_TILE * t + 128 * j, Q_TILE * t + 128 * (j + 1))
            drow[:, cols] = jnp.broadcast_to(dr, (8, 128))
            lb = jnp.broadcast_to(lr, (8, 128))
            for u in range(4):
                lrow[8 * u : 8 * u + 8, cols] = jnp.where(
                    ids > keyid[8 * u : 8 * u + 8, :], lb, HIDDEN
                )

    def tile(qi, ki):
        qs = pl.ds(pl.multiple_of(qi * Q_TILE, Q_TILE), Q_TILE)
        ks = pl.ds(pl.multiple_of(ki * K_TILE, K_TILE), K_TILE)
        q = qg[pl.ds(qi * 4, 4), 0:ROWS, :].reshape(Q_TILE, WIDTH)
        g = qg[pl.ds(qi * 4, 4), ROWS : 2 * ROWS, :].reshape(Q_TILE, WIDTH)
        k = kv[0, pl.ds(ki * 4, 4), :, :].reshape(K_TILE, WIDTH)
        v = kv[1, pl.ds(ki * 4, 4), :, :].reshape(K_TILE, WIDTH)
        s = lax.dot_general(k, q, NT, preferred_element_type=F32)
        dp = lax.dot_general(v, g, NT, preferred_element_type=F32)
        lr = lrow[pl.ds(pl.multiple_of(ki * 8, 8), 8), qs]
        bias = jnp.broadcast_to(lr[:, None, :], (8, BLK, Q_TILE)).reshape(K_TILE, Q_TILE)
        p = jnp.exp2(s * TO_EXP2 - bias)
        ds = (p * (dp - drow[0:1, qs])).astype(BF16)
        dv_acc[ks, :] += jnp.dot(p.astype(BF16), g, preferred_element_type=F32)
        dk_acc[ks, :] += jnp.dot(ds, q, preferred_element_type=F32)
        dq_acc[qs, :] += lax.dot_general(ds, k, TN, preferred_element_type=F32)

    dq_cps = {
        i: pltpu.make_async_remote_copy(
            src_ref=dq_send.at[i], dst_ref=dq_recv.at[i],
            send_sem=dq_ss.at[i], recv_sem=dq_rs.at[i],
            device_id=plane_dev(i, 1), device_id_type=MESH,
        )
        for i in range(1, 16)
    }
    sib_cps = {
        dz: pltpu.make_async_remote_copy(
            src_ref=sib_send.at[dz + 3], dst_ref=sib_recv.at[dz + 3],
            send_sem=sib_ss.at[dz + 3], recv_sem=sib_rs.at[dz + 3],
            device_id=sibling, device_id_type=MESH,
        )
        for dz in MINE
    }
    dkv_cps = {
        dz: pltpu.make_async_remote_copy(
            src_ref=dkv_send.at[dz + 3], dst_ref=dkv_recv.at[dz + 3],
            send_sem=dkv_ss.at[dz + 3], recv_sem=dkv_rs.at[dz + 3],
            device_id=line_dev(step, c), device_id_type=MESH,
        )
        for dz, step in {1: 1, -1: -1, 2: 2, -2: -2, 3: 2, -3: -2}.items()
    }
    for name, part, step in ((4, 0, 2), (5, 1, -2)):
        dkv_cps[name] = pltpu.make_async_remote_copy(
            src_ref=dkv_send.at[7, part], dst_ref=dkv_recv.at[7, part],
            send_sem=dkv_ss.at[name + 3], recv_sem=dkv_rs.at[name + 3],
            device_id=line_dev(step, c), device_id_type=MESH,
        )

    def queries_out(t):
        for i in range(4 * t, 4 * t + 4):
            if i > 0:
                dq_send[i] = dq_acc[i * ROWS : (i + 1) * ROWS, :].astype(BF16)
                dq_cps[i].start()

    def part(acc, i):
        return acc[i * ROWS : (i + 1) * ROWS, :]

    def to_sibling(dz):
        sib_send[dz + 3, 0] = part(dk_acc, THEIRS[dz]).astype(BF16)
        sib_send[dz + 3, 1] = part(dv_acc, THEIRS[dz]).astype(BF16)
        sib_cps[dz].start()

    def chip_sum(dz):
        sib_cps[dz].wait_recv()
        a = part(dk_acc, MINE[dz]) + sib_recv[dz + 3, 0].astype(F32)
        b = part(dv_acc, MINE[dz]) + sib_recv[dz + 3, 1].astype(F32)
        return a, b

    def to_owner(dz):
        a, b = chip_sum(dz)
        if dz in (1, -1):
            dkv_cps[3 * dz].wait_recv()
            a = a + dkv_recv[3 * dz + 3, 0].astype(F32)
            b = b + dkv_recv[3 * dz + 3, 1].astype(F32)
        if dz == 2:
            dkv_cps[4].wait_recv()
            a = a + dkv_recv[7, 0].astype(F32)
        if dz == -2:
            dkv_cps[5].wait_recv()
            b = b + dkv_recv[7, 1].astype(F32)
        dkv_send[dz + 3, 0] = a.astype(BF16)
        dkv_send[dz + 3, 1] = b.astype(BF16)
        dkv_cps[dz].start()
        if dz == 4:
            dkv_cps[5].start()

    def before(n):
        if n == 0:
            for offset in ((1, 0), (3, 0), (0, 1), (0, 3)):
                q_cps[at[offset]].wait_recv()
            for offset in ((1, 1), (3, 3), (1, 3), (3, 1)):
                q_cps[at[offset]].start()
            for dz in (1, -1):
                kz_cps[dz].wait_recv()
                kz_cps[3 * dz].start()
                kc_cps[dz].start()
            rows_of(0)
            kc_cps[0].wait_recv()
        if n == 1:
            for dz in (2, -2):
                kz_cps[dz].wait_recv()
                kz_cps[4 if dz == 2 else 5].start()
                kc_cps[dz].start()
            for offset in ((2, 0), (0, 2)):
                q_cps[at[offset]].wait_recv()
            for i in (at[1, 2], at[2, 1], at[3, 2], at[2, 3], far, 16):
                q_cps[i].start()
            kc_cps[1].wait_recv()
            kc_cps[-1].wait_recv()
        if n == 2:
            q_cps[at[1, 1]].wait_recv()
            rows_of(1)
        if n == 4:
            for dz in (3, -3):
                kz_cps[dz].wait_recv()
                kc_cps[dz].start()
            kc_cps[2].wait_recv()
            kc_cps[-2].wait_recv()
        if n == 5:
            kz_cps[4].wait_recv()
            kz_cps[5].wait_recv()
            kc_cps[4].start()
        if n == 6:
            for dz in (3, -3, 4):
                kc_cps[dz].wait_recv()
        if n == 8:
            queries_out(0)
            queries_out(1)
            for i in (8, 9, 10, 11, 16):
                q_cps[i].wait_recv()
            rows_of(2)
        if n == 9:
            for i in (12, 13, 14, 15):
                q_cps[i].wait_recv()
            rows_of(3)
        if n == 10:
            for dz in (4, 3, -3):
                to_sibling(dz)
        if n == 11:
            to_owner(4)
        if n == 12:
            to_owner(3)
            to_owner(-3)
            to_sibling(2)
            to_sibling(-2)
        if n == 14:
            queries_out(2)
        if n == 15:
            to_sibling(1)
            to_sibling(-1)
            to_owner(2)
            to_owner(-2)

    hooks = (0, 1, 2, 4, 5, 6, 8, 9, 10, 11, 12, 14, 15)

    def step(n, carry):
        for hook in hooks:
            pl.when(n == hook)(lambda hook=hook: before(hook))
        tile(pick([q for q, _ in TILES], n), pick([k for _, k in TILES], n))
        return carry

    lax.fori_loop(0, len(TILES), step, 0)

    to_sibling(0)
    queries_out(3)
    to_owner(1)
    to_owner(-1)

    a, b = chip_sum(0)
    total = dq_acc[0:ROWS, :]
    for i in range(1, 16):
        dq_cps[i].wait_recv()
        total = total + dq_recv[i].astype(F32)
    out[0] = (total * SCALE).astype(BF16)
    for dz in (2, -2, 1, -1):
        dkv_cps[dz].wait_recv()
        a = a + dkv_recv[dz + 3, 0].astype(F32)
        b = b + dkv_recv[dz + 3, 1].astype(F32)
    out[1] = (a * SCALE).astype(BF16)
    out[2] = b.astype(BF16)

    for group in (q_cps, kz_cps, kc_cps, dq_cps, dkv_cps, sib_cps):
        for cp in group.values():
            cp.wait_send()


def per_device(queries, keys_in, values_in, outputs_saved, out_grad, log_sum, block_table):
    hbm = pl.BlockSpec(memory_space=pl.ANY)
    vmem = pl.BlockSpec(memory_space=pltpu.VMEM)
    smem = pl.BlockSpec(memory_space=pltpu.SMEM)
    dma = pltpu.SemaphoreType.DMA
    sums = pl.pallas_call(
        kernel,
        out_shape=jax.ShapeDtypeStruct((3, ROWS, WIDTH), BF16),
        in_specs=[hbm, hbm, hbm, hbm, hbm, vmem, smem],
        out_specs=vmem,
        scratch_shapes=[
            pltpu.VMEM((16, CHUNK, WIDTH), BF16),
            pltpu.VMEM((2, 16, ROWS, WIDTH), BF16),
            pltpu.VMEM((ROWS, WIDTH), BF16),
            pltpu.VMEM((16 * ROWS, WIDTH), F32),
            pltpu.VMEM((16 * ROWS, WIDTH), F32),
            pltpu.VMEM((16 * ROWS, WIDTH), F32),
            pltpu.VMEM((32, 16 * ROWS), F32),
            pltpu.VMEM((8, 16 * ROWS), F32),
            pltpu.VMEM((32, 128), jnp.int32),
            pltpu.VMEM((16, ROWS, WIDTH), BF16),
            pltpu.VMEM((16, ROWS, WIDTH), BF16),
            pltpu.VMEM((8, 2, ROWS, WIDTH), BF16),
            pltpu.VMEM((8, 2, ROWS, WIDTH), BF16),
            pltpu.VMEM((8, 2, ROWS, WIDTH), BF16),
            pltpu.VMEM((8, 2, ROWS, WIDTH), BF16),
            dma((5,)), dma((17,)), dma((17,)), dma((9,)), dma((9,)), dma((8,)), dma((8,)),
            dma((16,)), dma((16,)), dma((8,)), dma((8,)), dma((9,)), dma((9,)),
        ],
        compiler_params=pltpu.CompilerParams(
            collective_id=0, has_side_effects=True, vmem_limit_bytes=60 << 20
        ),
    )(
        queries, keys_in, values_in, outputs_saved, out_grad,
        log_sum.reshape(1, ROWS), block_table,
    )
    return tuple(sums[i] for i in range(3))


def solution(mesh):
    rows = P(("pb", "ka"), None)
    return jax.shard_map(
        per_device,
        mesh=mesh,
        in_specs=(rows, rows, rows, rows, rows, P(("pb", "ka")), P()),
        out_specs=(rows, rows, rows),
        check_vma=False,
    )
```

```python
import math

import jax
import jax.numpy as jnp
from jax import lax
from jax.experimental import pallas as pl
from jax.experimental.pallas import tpu as pltpu
from jax.sharding import PartitionSpec as P

MESH = pl.DeviceIdType.MESH
F32, BF16 = jnp.float32, jnp.bfloat16
ROWS = 160
BLK = 80
WIDTH = 128
SCALE = 1.0 / math.sqrt(WIDTH)
TO_EXP2 = SCALE * math.log2(math.e)
LOG2E = math.log2(math.e)
HIDDEN = 1e30
CHUNK = 336
PLANE = (
    (0, 0), (1, 0), (3, 0), (0, 1), (0, 3), (2, 0), (0, 2), (1, 1),
    (2, 2), (2, 1), (2, 3), (1, 2), (3, 2), (3, 3), (1, 3), (3, 1),
)
LINE = (
    (0, 0), (1, 0), (-1, 0), (0, 1), (1, 1), (-1, 1), (2, 0), (-2, 0),
    (2, 1), (-2, 1), (3, 0), (-3, 0), (3, 1), (-3, 1), (4, 0), (4, 1),
)
MINE = {dz: LINE.index((dz, 0)) for dz in (0, 1, -1, 2, -2, 3, -3, 4)}
THEIRS = {dz: LINE.index((dz, 1)) for dz in (0, 1, -1, 2, -2, 3, -3, 4)}
TILES = (
    (0, 0), (0, 1), (1, 1), (1, 0), (1, 2), (0, 2), (2, 2), (2, 3),
    (3, 3), (0, 3), (1, 3), (3, 2), (2, 1), (2, 0), (3, 1), (3, 0),
)
Q_TILE, K_TILE = 4 * ROWS, 4 * ROWS
NT = (((1,), (1,)), ((), ()))
TN = (((0,), (0,)), ((), ()))


def place():
    pb, ka = lax.axis_index("pb"), lax.axis_index("ka")
    x, y, z, c = (ka // 2) % 4, ka // 8, (pb // 2) * 2 + ka % 2, pb % 2
    return x, y, z, c


def device(x, y, z, c):
    return ((z // 2) * 2 + c, y * 8 + x * 2 + z % 2)


def storage(x, y, z, c):
    pb, ka = device(x, y, z, c)
    return pb * 32 + ka


def kernel(
    q_in, k_in, v_in, o_in, g_in, l_in, table,
    out,
    qg, kv, o_own, dq_acc, dk_acc, dv_acc, lrow, drow, keyid,
    dq_send, dq_recv, sib_send, sib_recv, dkv_send, dkv_recv,
    local_sem, q_ss, q_rs, kz_ss, kz_rs, kc_ss, kc_rs,
    dq_ss, dq_rs, sib_ss, sib_rs, dkv_ss, dkv_rs,
):
    x, y, z, c = place()
    other = 1 - c

    def plane_dev(i, sign):
        dx, dy = PLANE[i]
        return device((x + sign * dx + 4) % 4, (y + sign * dy + 4) % 4, z, c)

    def line_dev(dz, core):
        return device(x, y, (z + dz + 8) % 8, core)

    sibling = device(x, y, z, other)
    partners = [plane_dev(PLANE.index(at), 1) for at in ((1, 0), (3, 0), (0, 1), (0, 3), (2, 0), (0, 2))]
    partners += [line_dev(dz, c) for dz in (1, -1, 2, -2)] + [sibling]
    barrier = pltpu.get_barrier_semaphore()
    for p in partners:
        pl.semaphore_signal(barrier, inc=1, device_id=p, device_id_type=MESH)

    loads = [
        pltpu.make_async_copy(k_in, kv.at[0, 0], local_sem.at[0]),
        pltpu.make_async_copy(v_in, kv.at[1, 0], local_sem.at[1]),
        pltpu.make_async_copy(g_in, qg.at[0, pl.ds(ROWS, ROWS)], local_sem.at[2]),
        pltpu.make_async_copy(o_in, o_own, local_sem.at[3]),
        pltpu.make_async_copy(q_in, qg.at[0, pl.ds(0, ROWS)], local_sem.at[4]),
    ]
    for cp in loads:
        cp.start()

    def q_copy(i, held, dx, dy, sem, rows=(0, CHUNK)):
        return pltpu.make_async_remote_copy(
            src_ref=qg.at[held, pl.ds(*rows)], dst_ref=qg.at[i, pl.ds(*rows)],
            send_sem=q_ss.at[sem], recv_sem=q_rs.at[sem],
            device_id=device((x - dx + 4) % 4, (y - dy + 4) % 4, z, c), device_id_type=MESH,
        )

    at = {offset: i for i, offset in enumerate(PLANE)}
    q_cps = {}
    for offset in ((1, 0), (3, 0), (0, 1), (0, 3), (2, 0), (0, 2)):
        q_cps[at[offset]] = q_copy(at[offset], 0, *offset, at[offset])
    for dx, dy in ((1, 1), (3, 3), (1, 2), (3, 2)):
        q_cps[at[dx, dy]] = q_copy(at[dx, dy], at[0, dy], dx, 0, at[dx, dy])
    for dx, dy in ((1, 3), (3, 1), (2, 1), (2, 3)):
        q_cps[at[dx, dy]] = q_copy(at[dx, dy], at[dx, 0], 0, dy, at[dx, dy])
    far = at[2, 2]
    q_cps[far] = q_copy(far, at[0, 2], 2, 0, far, (0, 176))
    q_cps[16] = q_copy(far, at[2, 0], 0, 2, 16, (176, CHUNK - 176))

    kz_cps = {}
    for dz, (held, step) in {
        1: (0, 1), -1: (0, -1), 2: (0, 2), -2: (0, -2), 3: (1, 2), -3: (-1, -2),
    }.items():
        kz_cps[dz] = pltpu.make_async_remote_copy(
            src_ref=kv.at[:, MINE[held]], dst_ref=kv.at[:, MINE[dz]],
            send_sem=kz_ss.at[dz + 3], recv_sem=kz_rs.at[dz + 3],
            device_id=line_dev(-step, c), device_id_type=MESH,
        )
    for name, part, step in ((4, 0, 2), (5, 1, -2)):
        kz_cps[name] = pltpu.make_async_remote_copy(
            src_ref=kv.at[part, MINE[step]], dst_ref=kv.at[part, MINE[4]],
            send_sem=kz_ss.at[name + 3], recv_sem=kz_rs.at[name + 3],
            device_id=line_dev(-step, c), device_id_type=MESH,
        )
    kc_cps = {
        dz: pltpu.make_async_remote_copy(
            src_ref=kv.at[:, MINE[dz]], dst_ref=kv.at[:, THEIRS[dz]],
            send_sem=kc_ss.at[dz + 3], recv_sem=kc_rs.at[dz + 3],
            device_id=sibling, device_id_type=MESH,
        )
        for dz in MINE
    }

    for cp in loads[:2]:
        cp.wait()
    pl.semaphore_wait(barrier, len(partners))
    for dz in (1, -1):
        kz_cps[dz].start()
    kc_cps[0].start()
    for dz in (2, -2):
        kz_cps[dz].start()

    for cp in loads[2:]:
        cp.wait()
    q0, g0 = qg[0, 0:ROWS, :], qg[0, ROWS : 2 * ROWS, :]
    k0, v0 = kv[0, 0], kv[1, 0]
    prod = g0.astype(F32) * o_own[...].astype(F32)
    high = prod.astype(BF16)
    low = (prod - high.astype(F32)).astype(BF16)
    ones = jnp.ones((8, WIDTH), BF16)
    delta8 = lax.dot_general(ones, high, NT, preferred_element_type=F32)
    delta8 += lax.dot_general(ones, low, NT, preferred_element_type=F32)
    delta = delta8[0:1, :]
    lse = l_in[...] * LOG2E
    sub = lax.broadcasted_iota(jnp.int32, (8, ROWS), 0)
    both = jnp.where(sub % 2 == 0, lse, delta)
    p1 = both.astype(BF16).astype(F32)
    p2 = (both - p1).astype(BF16).astype(F32)
    p3 = both - p1 - p2
    pieces = jnp.where(sub < 2, p1, jnp.where(sub < 4, p2, jnp.where(sub < 6, p3, 0.0)))
    wide = jnp.concatenate([pieces, jnp.zeros((8, 256 - ROWS), F32)], axis=1)
    first, rest = wide[:, 0:128], wide[:, 128:256]
    lane = lax.broadcasted_iota(jnp.int32, (8, 128), 1)
    second = jnp.where(
        lane < 48, pltpu.roll(first, 48, 1), pltpu.roll(rest, 48, 1)
    )
    keep = lane < BLK
    stats = jnp.concatenate(
        [jnp.where(keep, first, 0.0), jnp.where(keep, second, 0.0)], axis=0
    )
    qg[0, 2 * ROWS : CHUNK, :] = stats.astype(BF16)

    for offset in ((1, 0), (3, 0), (0, 1), (0, 3), (2, 0), (0, 2)):
        q_cps[at[offset]].start()
    dq_acc[...] = jnp.zeros_like(dq_acc)
    dk_acc[...] = jnp.zeros_like(dk_acc)
    dv_acc[...] = jnp.zeros_like(dv_acc)

    row = lax.broadcasted_iota(jnp.int32, (ROWS, ROWS), 0)
    col = lax.broadcasted_iota(jnp.int32, (ROWS, ROWS), 1)
    seen = (row <= col) & ((row >= BLK) == (col >= BLK))
    s0 = lax.dot_general(k0, q0, NT, preferred_element_type=F32)
    e0 = jnp.exp2(jnp.where(seen, s0 * TO_EXP2 - lse, -HIDDEN))
    dp0 = lax.dot_general(v0, g0, NT, preferred_element_type=F32)
    ds0 = (e0 * (dp0 - delta)).astype(BF16)
    dq_acc[0:ROWS, :] = lax.dot_general(ds0, k0, TN, preferred_element_type=F32)
    dk_acc[0:ROWS, :] = jnp.dot(ds0, q0, preferred_element_type=F32)
    dv_acc[0:ROWS, :] = jnp.dot(e0.astype(BF16), g0, preferred_element_type=F32)

    for r in range(32):
        dz, h = LINE[r // 2]
        entry = storage(x, y, (z + dz + 8) % 8, c if h == 0 else other) * 2 + r % 2
        keyid[r : r + 1, :] = jnp.full((1, 128), table[entry], jnp.int32)

    def rows_of(t):
        blocks = []
        for i in range(4 * t, 4 * t + 4):
            st = qg[i, 2 * ROWS : CHUNK, :].astype(F32)
            dx, dy = PLANE[i]
            entry = storage((x + dx) % 4, (y + dy) % 4, z, c) * 2
            blocks += [(st[0:8, :], table[entry]), (st[8:16, :], table[entry + 1])]
        for j in range(5):
            acc = jnp.zeros((8, 128), F32)
            ids = jnp.zeros((8, 128), jnp.int32)
            for r, (st, entry) in enumerate(blocks):
                shift = BLK * r - 128 * j
                if shift <= -BLK or shift >= 128:
                    continue
                here = (lane >= max(shift, 0)) & (lane < min(128, shift + BLK))
                moved = st if shift % 128 == 0 else pltpu.roll(st, shift % 128, 1)
                acc = jnp.where(here, moved, acc)
                ids = jnp.where(here, entry, ids)
            lr = acc[0:1, :] + acc[2:3, :] + acc[4:5, :]
            dr = acc[1:2, :] + acc[3:4, :] + acc[5:6, :]
            cols = slice(Q_TILE * t + 128 * j, Q_TILE * t + 128 * (j + 1))
            drow[:, cols] = jnp.broadcast_to(dr, (8, 128))
            lb = jnp.broadcast_to(lr, (8, 128))
            for u in range(4):
                lrow[8 * u : 8 * u + 8, cols] = jnp.where(
                    ids > keyid[8 * u : 8 * u + 8, :], lb, HIDDEN
                )

    def tile(qi, ki):
        qs = pl.ds(qi * Q_TILE, Q_TILE)
        ks = pl.ds(ki * K_TILE, K_TILE)
        q = qg[pl.ds(qi * 4, 4), 0:ROWS, :].reshape(Q_TILE, WIDTH)
        g = qg[pl.ds(qi * 4, 4), ROWS : 2 * ROWS, :].reshape(Q_TILE, WIDTH)
        k = kv[0, pl.ds(ki * 4, 4), :, :].reshape(K_TILE, WIDTH)
        v = kv[1, pl.ds(ki * 4, 4), :, :].reshape(K_TILE, WIDTH)
        s = lax.dot_general(k, q, NT, preferred_element_type=F32)
        dp = lax.dot_general(v, g, NT, preferred_element_type=F32)
        lr = lrow[pl.ds(ki * 8, 8), qs]
        bias = jnp.broadcast_to(lr[:, None, :], (8, BLK, Q_TILE)).reshape(K_TILE, Q_TILE)
        p = jnp.exp2(s * TO_EXP2 - bias)
        ds = (p * (dp - drow[0:1, qs])).astype(BF16)
        dv_acc[ks, :] += jnp.dot(p.astype(BF16), g, preferred_element_type=F32)
        dk_acc[ks, :] += jnp.dot(ds, q, preferred_element_type=F32)
        dq_acc[qs, :] += lax.dot_general(ds, k, TN, preferred_element_type=F32)

    dq_cps = {
        i: pltpu.make_async_remote_copy(
            src_ref=dq_send.at[i], dst_ref=dq_recv.at[i],
            send_sem=dq_ss.at[i], recv_sem=dq_rs.at[i],
            device_id=plane_dev(i, 1), device_id_type=MESH,
        )
        for i in range(1, 16)
    }
    sib_cps = {
        dz: pltpu.make_async_remote_copy(
            src_ref=sib_send.at[dz + 3], dst_ref=sib_recv.at[dz + 3],
            send_sem=sib_ss.at[dz + 3], recv_sem=sib_rs.at[dz + 3],
            device_id=sibling, device_id_type=MESH,
        )
        for dz in MINE
    }
    dkv_cps = {
        dz: pltpu.make_async_remote_copy(
            src_ref=dkv_send.at[dz + 3], dst_ref=dkv_recv.at[dz + 3],
            send_sem=dkv_ss.at[dz + 3], recv_sem=dkv_rs.at[dz + 3],
            device_id=line_dev(step, c), device_id_type=MESH,
        )
        for dz, step in {1: 1, -1: -1, 2: 2, -2: -2, 3: 2, -3: -2}.items()
    }
    for name, part, step in ((4, 0, 2), (5, 1, -2)):
        dkv_cps[name] = pltpu.make_async_remote_copy(
            src_ref=dkv_send.at[7, part], dst_ref=dkv_recv.at[7, part],
            send_sem=dkv_ss.at[name + 3], recv_sem=dkv_rs.at[name + 3],
            device_id=line_dev(step, c), device_id_type=MESH,
        )

    def queries_out(t):
        for i in range(4 * t, 4 * t + 4):
            if i > 0:
                dq_send[i] = dq_acc[i * ROWS : (i + 1) * ROWS, :].astype(BF16)
                dq_cps[i].start()

    def part(acc, i):
        return acc[i * ROWS : (i + 1) * ROWS, :]

    def to_sibling(dz):
        sib_send[dz + 3, 0] = part(dk_acc, THEIRS[dz]).astype(BF16)
        sib_send[dz + 3, 1] = part(dv_acc, THEIRS[dz]).astype(BF16)
        sib_cps[dz].start()

    def chip_sum(dz):
        sib_cps[dz].wait_recv()
        a = part(dk_acc, MINE[dz]) + sib_recv[dz + 3, 0].astype(F32)
        b = part(dv_acc, MINE[dz]) + sib_recv[dz + 3, 1].astype(F32)
        return a, b

    def to_owner(dz):
        a, b = chip_sum(dz)
        if dz in (1, -1):
            dkv_cps[3 * dz].wait_recv()
            a = a + dkv_recv[3 * dz + 3, 0].astype(F32)
            b = b + dkv_recv[3 * dz + 3, 1].astype(F32)
        if dz == 2:
            dkv_cps[4].wait_recv()
            a = a + dkv_recv[7, 0].astype(F32)
        if dz == -2:
            dkv_cps[5].wait_recv()
            b = b + dkv_recv[7, 1].astype(F32)
        dkv_send[dz + 3, 0] = a.astype(BF16)
        dkv_send[dz + 3, 1] = b.astype(BF16)
        dkv_cps[dz].start()
        if dz == 4:
            dkv_cps[5].start()

    def before(n):
        if n == 0:
            for offset in ((1, 0), (3, 0), (0, 1), (0, 3)):
                q_cps[at[offset]].wait_recv()
            for offset in ((1, 1), (3, 3), (1, 3), (3, 1)):
                q_cps[at[offset]].start()
            for dz in (1, -1):
                kz_cps[dz].wait_recv()
                kz_cps[3 * dz].start()
                kc_cps[dz].start()
            rows_of(0)
            kc_cps[0].wait_recv()
        if n == 1:
            for dz in (2, -2):
                kz_cps[dz].wait_recv()
                kz_cps[4 if dz == 2 else 5].start()
                kc_cps[dz].start()
            for offset in ((2, 0), (0, 2)):
                q_cps[at[offset]].wait_recv()
            for i in (at[1, 2], at[2, 1], at[3, 2], at[2, 3], far, 16):
                q_cps[i].start()
            kc_cps[1].wait_recv()
            kc_cps[-1].wait_recv()
        if n == 2:
            q_cps[at[1, 1]].wait_recv()
            rows_of(1)
        if n == 4:
            for dz in (3, -3):
                kz_cps[dz].wait_recv()
                kc_cps[dz].start()
            kc_cps[2].wait_recv()
            kc_cps[-2].wait_recv()
        if n == 6:
            kz_cps[4].wait_recv()
            kz_cps[5].wait_recv()
            kc_cps[4].start()
            for i in (8, 9, 10, 11, 16):
                q_cps[i].wait_recv()
            rows_of(2)
        if n == 7:
            for dz in (3, -3, 4):
                kc_cps[dz].wait_recv()
        if n == 8:
            for i in (12, 13, 14, 15):
                q_cps[i].wait_recv()
            rows_of(3)
        if n == 11:
            for dz in (4, 3, -3):
                to_sibling(dz)
            queries_out(0)
            queries_out(1)
        if n == 12:
            for dz in (4, 3, -3):
                to_owner(dz)
            to_sibling(2)
            to_sibling(-2)
        if n == 14:
            queries_out(2)
        if n == 15:
            to_sibling(1)
            to_sibling(-1)


    for n, (qi, ki) in enumerate(TILES):
        before(n)
        tile(qi, ki)

    to_sibling(0)
    queries_out(3)
    for dz in (2, -2, 1, -1):
        to_owner(dz)

    a, b = chip_sum(0)
    total = dq_acc[0:ROWS, :]
    for i in range(1, 16):
        dq_cps[i].wait_recv()
        total = total + dq_recv[i].astype(F32)
    out[0] = (total * SCALE).astype(BF16)
    for dz in (2, -2, 1, -1):
        dkv_cps[dz].wait_recv()
        a = a + dkv_recv[dz + 3, 0].astype(F32)
        b = b + dkv_recv[dz + 3, 1].astype(F32)
    out[1] = (a * SCALE).astype(BF16)
    out[2] = b.astype(BF16)

    for group in (q_cps, kz_cps, kc_cps, dq_cps, dkv_cps, sib_cps):
        for cp in group.values():
            cp.wait_send()


def per_device(queries, keys_in, values_in, outputs_saved, out_grad, log_sum, block_table):
    hbm = pl.BlockSpec(memory_space=pl.ANY)
    vmem = pl.BlockSpec(memory_space=pltpu.VMEM)
    smem = pl.BlockSpec(memory_space=pltpu.SMEM)
    dma = pltpu.SemaphoreType.DMA
    sums = pl.pallas_call(
        kernel,
        out_shape=jax.ShapeDtypeStruct((3, ROWS, WIDTH), BF16),
        in_specs=[hbm, hbm, hbm, hbm, hbm, vmem, smem],
        out_specs=vmem,
        scratch_shapes=[
            pltpu.VMEM((16, CHUNK, WIDTH), BF16),
            pltpu.VMEM((2, 16, ROWS, WIDTH), BF16),
            pltpu.VMEM((ROWS, WIDTH), BF16),
            pltpu.VMEM((16 * ROWS, WIDTH), F32),
            pltpu.VMEM((16 * ROWS, WIDTH), F32),
            pltpu.VMEM((16 * ROWS, WIDTH), F32),
            pltpu.VMEM((32, 16 * ROWS), F32),
            pltpu.VMEM((8, 16 * ROWS), F32),
            pltpu.VMEM((32, 128), jnp.int32),
            pltpu.VMEM((16, ROWS, WIDTH), BF16),
            pltpu.VMEM((16, ROWS, WIDTH), BF16),
            pltpu.VMEM((8, 2, ROWS, WIDTH), BF16),
            pltpu.VMEM((8, 2, ROWS, WIDTH), BF16),
            pltpu.VMEM((8, 2, ROWS, WIDTH), BF16),
            pltpu.VMEM((8, 2, ROWS, WIDTH), BF16),
            dma((5,)), dma((17,)), dma((17,)), dma((9,)), dma((9,)), dma((8,)), dma((8,)),
            dma((16,)), dma((16,)), dma((8,)), dma((8,)), dma((9,)), dma((9,)),
        ],
        compiler_params=pltpu.CompilerParams(
            collective_id=0, has_side_effects=True, vmem_limit_bytes=60 << 20
        ),
    )(
        queries, keys_in, values_in, outputs_saved, out_grad,
        log_sum.reshape(1, ROWS), block_table,
    )
    return tuple(sums[i] for i in range(3))


def solution(mesh):
    rows = P(("pb", "ka"), None)
    return jax.shard_map(
        per_device,
        mesh=mesh,
        in_specs=(rows, rows, rows, rows, rows, P(("pb", "ka")), P()),
        out_specs=(rows, rows, rows),
        check_vma=False,
    )
```

```python
import math

import jax
import jax.numpy as jnp
from jax import lax
from jax.experimental import pallas as pl
from jax.experimental.pallas import tpu as pltpu
from jax.sharding import PartitionSpec as P

MESH = pl.DeviceIdType.MESH
F32, BF16 = jnp.float32, jnp.bfloat16
ROWS = 160
BLK = 80
WIDTH = 128
SCALE = 1.0 / math.sqrt(WIDTH)
TO_EXP2 = SCALE * math.log2(math.e)
LOG2E = math.log2(math.e)
HIDDEN = 1e30
CHUNK = 336
PLANE = (
    (0, 0), (1, 0), (3, 0), (0, 1), (0, 3), (2, 0), (0, 2), (1, 1),
    (2, 2), (2, 1), (2, 3), (1, 2), (3, 2), (3, 3), (1, 3), (3, 1),
)
LINE = (
    (0, 0), (1, 0), (-1, 0), (0, 1), (1, 1), (-1, 1), (2, 0), (-2, 0),
    (2, 1), (-2, 1), (3, 0), (-3, 0), (3, 1), (-3, 1), (4, 0), (4, 1),
)
MINE = {dz: LINE.index((dz, 0)) for dz in (0, 1, -1, 2, -2, 3, -3, 4)}
THEIRS = {dz: LINE.index((dz, 1)) for dz in (0, 1, -1, 2, -2, 3, -3, 4)}
TILES = (
    (0, 0), (0, 1), (1, 1), (1, 0), (1, 2), (0, 2), (2, 2), (2, 3),
    (3, 3), (0, 3), (1, 3), (3, 2), (2, 1), (2, 0), (3, 1), (3, 0),
)
Q_TILE, K_TILE = 4 * ROWS, 4 * ROWS
NT = (((1,), (1,)), ((), ()))
TN = (((0,), (0,)), ((), ()))


def place():
    pb, ka = lax.axis_index("pb"), lax.axis_index("ka")
    x, y, z, c = (ka // 2) % 4, ka // 8, (pb // 2) * 2 + ka % 2, pb % 2
    return x, y, z, c


def device(x, y, z, c):
    return ((z // 2) * 2 + c, y * 8 + x * 2 + z % 2)


def storage(x, y, z, c):
    pb, ka = device(x, y, z, c)
    return pb * 32 + ka


def kernel(
    q_in, k_in, v_in, o_in, g_in, l_in, table_in,
    out,
    qg, kv, o_own, l_own, table, dq_acc, dk_acc, dv_acc, lrow, drow, keyid,
    dq_send, dq_recv, sib_send, sib_recv, dkv_send, dkv_recv,
    local_sem, q_ss, q_rs, kz_ss, kz_rs, kc_ss, kc_rs,
    dq_ss, dq_rs, sib_ss, sib_rs, dkv_ss, dkv_rs,
):
    x, y, z, c = place()
    other = 1 - c

    def plane_dev(i, sign):
        dx, dy = PLANE[i]
        return device((x + sign * dx + 4) % 4, (y + sign * dy + 4) % 4, z, c)

    def line_dev(dz, core):
        return device(x, y, (z + dz + 8) % 8, core)

    sibling = device(x, y, z, other)
    partners = [plane_dev(PLANE.index(at), 1) for at in ((1, 0), (3, 0), (0, 1), (0, 3), (2, 0), (0, 2))]
    partners += [line_dev(dz, c) for dz in (1, -1, 2, -2)] + [sibling]
    barrier = pltpu.get_barrier_semaphore()
    for p in partners:
        pl.semaphore_signal(barrier, inc=1, device_id=p, device_id_type=MESH)

    loads = [
        pltpu.make_async_copy(k_in, kv.at[0, 0], local_sem.at[0]),
        pltpu.make_async_copy(v_in, kv.at[1, 0], local_sem.at[1]),
        pltpu.make_async_copy(g_in, qg.at[0, pl.ds(ROWS, ROWS)], local_sem.at[2]),
        pltpu.make_async_copy(o_in, o_own, local_sem.at[3]),
        pltpu.make_async_copy(q_in, qg.at[0, pl.ds(0, ROWS)], local_sem.at[4]),
        pltpu.make_async_copy(l_in, l_own, local_sem.at[5]),
        pltpu.make_async_copy(table_in, table, local_sem.at[6]),
    ]
    for cp in loads:
        cp.start()

    def q_copy(i, held, dx, dy, sem, rows=(0, CHUNK)):
        return pltpu.make_async_remote_copy(
            src_ref=qg.at[held, pl.ds(*rows)], dst_ref=qg.at[i, pl.ds(*rows)],
            send_sem=q_ss.at[sem], recv_sem=q_rs.at[sem],
            device_id=device((x - dx + 4) % 4, (y - dy + 4) % 4, z, c), device_id_type=MESH,
        )

    at = {offset: i for i, offset in enumerate(PLANE)}
    q_cps = {}
    for offset in ((1, 0), (3, 0), (0, 1), (0, 3), (2, 0), (0, 2)):
        q_cps[at[offset]] = q_copy(at[offset], 0, *offset, at[offset])
    for dx, dy in ((1, 1), (3, 3), (1, 2), (3, 2)):
        q_cps[at[dx, dy]] = q_copy(at[dx, dy], at[0, dy], dx, 0, at[dx, dy])
    for dx, dy in ((1, 3), (3, 1), (2, 1), (2, 3)):
        q_cps[at[dx, dy]] = q_copy(at[dx, dy], at[dx, 0], 0, dy, at[dx, dy])
    far = at[2, 2]
    q_cps[far] = q_copy(far, at[0, 2], 2, 0, far, (0, 176))
    q_cps[16] = q_copy(far, at[2, 0], 0, 2, 16, (176, CHUNK - 176))

    kz_cps = {}
    for dz, (held, step) in {
        1: (0, 1), -1: (0, -1), 2: (0, 2), -2: (0, -2), 3: (1, 2), -3: (-1, -2),
    }.items():
        kz_cps[dz] = pltpu.make_async_remote_copy(
            src_ref=kv.at[:, MINE[held]], dst_ref=kv.at[:, MINE[dz]],
            send_sem=kz_ss.at[dz + 3], recv_sem=kz_rs.at[dz + 3],
            device_id=line_dev(-step, c), device_id_type=MESH,
        )
    for name, part, step in ((4, 0, 2), (5, 1, -2)):
        kz_cps[name] = pltpu.make_async_remote_copy(
            src_ref=kv.at[part, MINE[step]], dst_ref=kv.at[part, MINE[4]],
            send_sem=kz_ss.at[name + 3], recv_sem=kz_rs.at[name + 3],
            device_id=line_dev(-step, c), device_id_type=MESH,
        )
    kc_cps = {
        dz: pltpu.make_async_remote_copy(
            src_ref=kv.at[:, MINE[dz]], dst_ref=kv.at[:, THEIRS[dz]],
            send_sem=kc_ss.at[dz + 3], recv_sem=kc_rs.at[dz + 3],
            device_id=sibling, device_id_type=MESH,
        )
        for dz in MINE
    }

    for cp in loads[:2]:
        cp.wait()
    pl.semaphore_wait(barrier, len(partners))
    for dz in (1, -1):
        kz_cps[dz].start()
    kc_cps[0].start()
    for dz in (2, -2):
        kz_cps[dz].start()

    for cp in loads[2:]:
        cp.wait()
    q0, g0 = qg[0, 0:ROWS, :], qg[0, ROWS : 2 * ROWS, :]
    k0, v0 = kv[0, 0], kv[1, 0]
    prod = g0.astype(F32) * o_own[...].astype(F32)
    high = prod.astype(BF16)
    low = (prod - high.astype(F32)).astype(BF16)
    ones = jnp.ones((8, WIDTH), BF16)
    delta8 = lax.dot_general(ones, high, NT, preferred_element_type=F32)
    delta8 += lax.dot_general(ones, low, NT, preferred_element_type=F32)
    delta = delta8[0:1, :]
    lse = l_own[...] * LOG2E
    sub = lax.broadcasted_iota(jnp.int32, (8, ROWS), 0)
    both = jnp.where(sub % 2 == 0, lse, delta)
    p1 = both.astype(BF16).astype(F32)
    p2 = (both - p1).astype(BF16).astype(F32)
    p3 = both - p1 - p2
    pieces = jnp.where(sub < 2, p1, jnp.where(sub < 4, p2, jnp.where(sub < 6, p3, 0.0)))
    wide = jnp.concatenate([pieces, jnp.zeros((8, 256 - ROWS), F32)], axis=1)
    first, rest = wide[:, 0:128], wide[:, 128:256]
    lane = lax.broadcasted_iota(jnp.int32, (8, 128), 1)
    second = jnp.where(
        lane < 48, pltpu.roll(first, 48, 1), pltpu.roll(rest, 48, 1)
    )
    keep = lane < BLK
    stats = jnp.concatenate(
        [jnp.where(keep, first, 0.0), jnp.where(keep, second, 0.0)], axis=0
    )
    qg[0, 2 * ROWS : CHUNK, :] = stats.astype(BF16)

    for offset in ((1, 0), (3, 0), (0, 1), (0, 3), (2, 0), (0, 2)):
        q_cps[at[offset]].start()
    dq_acc[...] = jnp.zeros_like(dq_acc)
    dk_acc[...] = jnp.zeros_like(dk_acc)
    dv_acc[...] = jnp.zeros_like(dv_acc)

    row = lax.broadcasted_iota(jnp.int32, (ROWS, ROWS), 0)
    col = lax.broadcasted_iota(jnp.int32, (ROWS, ROWS), 1)
    seen = (row <= col) & ((row >= BLK) == (col >= BLK))
    s0 = lax.dot_general(k0, q0, NT, preferred_element_type=F32)
    e0 = jnp.exp2(jnp.where(seen, s0 * TO_EXP2 - lse, -HIDDEN))
    dp0 = lax.dot_general(v0, g0, NT, preferred_element_type=F32)
    ds0 = (e0 * (dp0 - delta)).astype(BF16)
    dq_acc[0:ROWS, :] = lax.dot_general(ds0, k0, TN, preferred_element_type=F32)
    dk_acc[0:ROWS, :] = jnp.dot(ds0, q0, preferred_element_type=F32)
    dv_acc[0:ROWS, :] = jnp.dot(e0.astype(BF16), g0, preferred_element_type=F32)

    for r in range(32):
        dz, h = LINE[r // 2]
        entry = storage(x, y, (z + dz + 8) % 8, c if h == 0 else other) * 2 + r % 2
        keyid[r : r + 1, :] = jnp.full((1, 128), table[entry], jnp.int32)

    def rows_of(t):
        blocks = []
        for i in range(4 * t, 4 * t + 4):
            st = qg[i, 2 * ROWS : CHUNK, :].astype(F32)
            dx, dy = PLANE[i]
            entry = storage((x + dx) % 4, (y + dy) % 4, z, c) * 2
            blocks += [(st[0:8, :], table[entry]), (st[8:16, :], table[entry + 1])]
        for j in range(5):
            acc = jnp.zeros((8, 128), F32)
            ids = jnp.zeros((8, 128), jnp.int32)
            for r, (st, entry) in enumerate(blocks):
                shift = BLK * r - 128 * j
                if shift <= -BLK or shift >= 128:
                    continue
                here = (lane >= max(shift, 0)) & (lane < min(128, shift + BLK))
                moved = st if shift % 128 == 0 else pltpu.roll(st, shift % 128, 1)
                acc = jnp.where(here, moved, acc)
                ids = jnp.where(here, entry, ids)
            lr = acc[0:1, :] + acc[2:3, :] + acc[4:5, :]
            dr = acc[1:2, :] + acc[3:4, :] + acc[5:6, :]
            cols = slice(Q_TILE * t + 128 * j, Q_TILE * t + 128 * (j + 1))
            drow[:, cols] = jnp.broadcast_to(dr, (8, 128))
            lb = jnp.broadcast_to(lr, (8, 128))
            for u in range(4):
                lrow[8 * u : 8 * u + 8, cols] = jnp.where(
                    ids > keyid[8 * u : 8 * u + 8, :], lb, HIDDEN
                )

    def tile(qi, ki):
        qs = pl.ds(qi * Q_TILE, Q_TILE)
        ks = pl.ds(ki * K_TILE, K_TILE)
        q = qg[pl.ds(qi * 4, 4), 0:ROWS, :].reshape(Q_TILE, WIDTH)
        g = qg[pl.ds(qi * 4, 4), ROWS : 2 * ROWS, :].reshape(Q_TILE, WIDTH)
        k = kv[0, pl.ds(ki * 4, 4), :, :].reshape(K_TILE, WIDTH)
        v = kv[1, pl.ds(ki * 4, 4), :, :].reshape(K_TILE, WIDTH)
        s = lax.dot_general(k, q, NT, preferred_element_type=F32)
        dp = lax.dot_general(v, g, NT, preferred_element_type=F32)
        lr = lrow[pl.ds(ki * 8, 8), qs]
        bias = jnp.broadcast_to(lr[:, None, :], (8, BLK, Q_TILE)).reshape(K_TILE, Q_TILE)
        p = jnp.exp2(s * TO_EXP2 - bias)
        ds = (p * (dp - drow[0:1, qs])).astype(BF16)
        dv_acc[ks, :] += jnp.dot(p.astype(BF16), g, preferred_element_type=F32)
        dk_acc[ks, :] += jnp.dot(ds, q, preferred_element_type=F32)
        dq_acc[qs, :] += lax.dot_general(ds, k, TN, preferred_element_type=F32)

    dq_cps = {
        i: pltpu.make_async_remote_copy(
            src_ref=dq_send.at[i], dst_ref=dq_recv.at[i],
            send_sem=dq_ss.at[i], recv_sem=dq_rs.at[i],
            device_id=plane_dev(i, 1), device_id_type=MESH,
        )
        for i in range(1, 16)
    }
    sib_cps = {
        dz: pltpu.make_async_remote_copy(
            src_ref=sib_send.at[dz + 3], dst_ref=sib_recv.at[dz + 3],
            send_sem=sib_ss.at[dz + 3], recv_sem=sib_rs.at[dz + 3],
            device_id=sibling, device_id_type=MESH,
        )
        for dz in MINE
    }
    dkv_cps = {
        dz: pltpu.make_async_remote_copy(
            src_ref=dkv_send.at[dz + 3], dst_ref=dkv_recv.at[dz + 3],
            send_sem=dkv_ss.at[dz + 3], recv_sem=dkv_rs.at[dz + 3],
            device_id=line_dev(step, c), device_id_type=MESH,
        )
        for dz, step in {1: 1, -1: -1, 2: 2, -2: -2, 3: 2, -3: -2}.items()
    }
    for name, part, step in ((4, 0, 2), (5, 1, -2)):
        dkv_cps[name] = pltpu.make_async_remote_copy(
            src_ref=dkv_send.at[7, part], dst_ref=dkv_recv.at[7, part],
            send_sem=dkv_ss.at[name + 3], recv_sem=dkv_rs.at[name + 3],
            device_id=line_dev(step, c), device_id_type=MESH,
        )

    def queries_out(t):
        for i in range(4 * t, 4 * t + 4):
            if i > 0:
                dq_send[i] = dq_acc[i * ROWS : (i + 1) * ROWS, :].astype(BF16)
                dq_cps[i].start()

    def part(acc, i):
        return acc[i * ROWS : (i + 1) * ROWS, :]

    def to_sibling(dz):
        sib_send[dz + 3, 0] = part(dk_acc, THEIRS[dz]).astype(BF16)
        sib_send[dz + 3, 1] = part(dv_acc, THEIRS[dz]).astype(BF16)
        sib_cps[dz].start()

    def chip_sum(dz):
        sib_cps[dz].wait_recv()
        a = part(dk_acc, MINE[dz]) + sib_recv[dz + 3, 0].astype(F32)
        b = part(dv_acc, MINE[dz]) + sib_recv[dz + 3, 1].astype(F32)
        return a, b

    def to_owner(dz):
        a, b = chip_sum(dz)
        if dz in (1, -1):
            dkv_cps[3 * dz].wait_recv()
            a = a + dkv_recv[3 * dz + 3, 0].astype(F32)
            b = b + dkv_recv[3 * dz + 3, 1].astype(F32)
        if dz == 2:
            dkv_cps[4].wait_recv()
            a = a + dkv_recv[7, 0].astype(F32)
        if dz == -2:
            dkv_cps[5].wait_recv()
            b = b + dkv_recv[7, 1].astype(F32)
        dkv_send[dz + 3, 0] = a.astype(BF16)
        dkv_send[dz + 3, 1] = b.astype(BF16)
        dkv_cps[dz].start()
        if dz == 4:
            dkv_cps[5].start()

    def before(n):
        if n == 0:
            for offset in ((1, 0), (3, 0), (0, 1), (0, 3)):
                q_cps[at[offset]].wait_recv()
            for offset in ((1, 1), (3, 3), (1, 3), (3, 1)):
                q_cps[at[offset]].start()
            for dz in (1, -1):
                kz_cps[dz].wait_recv()
                kz_cps[3 * dz].start()
                kc_cps[dz].start()
            rows_of(0)
            kc_cps[0].wait_recv()
        if n == 1:
            for dz in (2, -2):
                kz_cps[dz].wait_recv()
                kz_cps[4 if dz == 2 else 5].start()
                kc_cps[dz].start()
            for offset in ((2, 0), (0, 2)):
                q_cps[at[offset]].wait_recv()
            for i in (at[1, 2], at[2, 1], at[3, 2], at[2, 3], far, 16):
                q_cps[i].start()
            kc_cps[1].wait_recv()
            kc_cps[-1].wait_recv()
        if n == 2:
            q_cps[at[1, 1]].wait_recv()
            rows_of(1)
        if n == 4:
            for dz in (3, -3):
                kz_cps[dz].wait_recv()
                kc_cps[dz].start()
            kc_cps[2].wait_recv()
            kc_cps[-2].wait_recv()
        if n == 6:
            kz_cps[4].wait_recv()
            kz_cps[5].wait_recv()
            kc_cps[4].start()
            for i in (8, 9, 10, 11, 16):
                q_cps[i].wait_recv()
            rows_of(2)
        if n == 7:
            for dz in (3, -3, 4):
                kc_cps[dz].wait_recv()
        if n == 8:
            for i in (12, 13, 14, 15):
                q_cps[i].wait_recv()
            rows_of(3)
        if n == 11:
            for dz in (4, 3, -3):
                to_sibling(dz)
            queries_out(0)
            queries_out(1)
        if n == 12:
            for dz in (4, 3, -3):
                to_owner(dz)
            to_sibling(2)
            to_sibling(-2)
        if n == 14:
            queries_out(2)
        if n == 15:
            to_sibling(1)
            to_sibling(-1)


    for n, (qi, ki) in enumerate(TILES):
        before(n)
        tile(qi, ki)

    to_sibling(0)
    queries_out(3)
    for dz in (2, -2, 1, -1):
        to_owner(dz)

    a, b = chip_sum(0)
    total = dq_acc[0:ROWS, :]
    for i in range(1, 16):
        dq_cps[i].wait_recv()
        total = total + dq_recv[i].astype(F32)
    out[0] = (total * SCALE).astype(BF16)
    for dz in (2, -2, 1, -1):
        dkv_cps[dz].wait_recv()
        a = a + dkv_recv[dz + 3, 0].astype(F32)
        b = b + dkv_recv[dz + 3, 1].astype(F32)
    out[1] = (a * SCALE).astype(BF16)
    out[2] = b.astype(BF16)

    for group in (q_cps, kz_cps, kc_cps, dq_cps, dkv_cps, sib_cps):
        for cp in group.values():
            cp.wait_send()


def per_device(queries, keys_in, values_in, outputs_saved, out_grad, log_sum, block_table):
    hbm = pl.BlockSpec(memory_space=pl.ANY)
    vmem = pl.BlockSpec(memory_space=pltpu.VMEM)
    dma = pltpu.SemaphoreType.DMA
    sums = pl.pallas_call(
        kernel,
        out_shape=jax.ShapeDtypeStruct((3, ROWS, WIDTH), BF16),
        in_specs=[hbm] * 7,
        out_specs=vmem,
        scratch_shapes=[
            pltpu.VMEM((16, CHUNK, WIDTH), BF16),
            pltpu.VMEM((2, 16, ROWS, WIDTH), BF16),
            pltpu.VMEM((ROWS, WIDTH), BF16),
            pltpu.VMEM((1, ROWS), F32),
            pltpu.SMEM((512,), jnp.int32),
            pltpu.VMEM((16 * ROWS, WIDTH), F32),
            pltpu.VMEM((16 * ROWS, WIDTH), F32),
            pltpu.VMEM((16 * ROWS, WIDTH), F32),
            pltpu.VMEM((32, 16 * ROWS), F32),
            pltpu.VMEM((8, 16 * ROWS), F32),
            pltpu.VMEM((32, 128), jnp.int32),
            pltpu.VMEM((16, ROWS, WIDTH), BF16),
            pltpu.VMEM((16, ROWS, WIDTH), BF16),
            pltpu.VMEM((8, 2, ROWS, WIDTH), BF16),
            pltpu.VMEM((8, 2, ROWS, WIDTH), BF16),
            pltpu.VMEM((8, 2, ROWS, WIDTH), BF16),
            pltpu.VMEM((8, 2, ROWS, WIDTH), BF16),
            dma((7,)), dma((17,)), dma((17,)), dma((9,)), dma((9,)), dma((8,)), dma((8,)),
            dma((16,)), dma((16,)), dma((8,)), dma((8,)), dma((9,)), dma((9,)),
        ],
        compiler_params=pltpu.CompilerParams(
            collective_id=0, has_side_effects=True, vmem_limit_bytes=60 << 20
        ),
    )(
        queries, keys_in, values_in, outputs_saved, out_grad,
        log_sum.reshape(1, ROWS), block_table,
    )
    return tuple(sums[i] for i in range(3))


def solution(mesh):
    rows = P(("pb", "ka"), None)
    return jax.shard_map(
        per_device,
        mesh=mesh,
        in_specs=(rows, rows, rows, rows, rows, P(("pb", "ka")), P()),
        out_specs=(rows, rows, rows),
        check_vma=False,
    )
```

```python
import math

import jax
import jax.numpy as jnp
from jax import lax
from jax.experimental import pallas as pl
from jax.experimental.pallas import tpu as pltpu
from jax.sharding import PartitionSpec as P

MESH = pl.DeviceIdType.MESH
F32, BF16 = jnp.float32, jnp.bfloat16
ROWS = 160
BLK = 80
WIDTH = 128
SCALE = 1.0 / math.sqrt(WIDTH)
TO_EXP2 = SCALE * math.log2(math.e)
LOG2E = math.log2(math.e)
HIDDEN = 1e30
CHUNK = 336
PLANE = (
    (0, 0), (1, 0), (3, 0), (0, 1), (0, 3), (2, 0), (0, 2), (1, 1),
    (2, 2), (2, 1), (2, 3), (1, 2), (3, 2), (3, 3), (1, 3), (3, 1),
)
LINE = (
    (0, 0), (1, 0), (-1, 0), (0, 1), (1, 1), (-1, 1), (2, 0), (-2, 0),
    (2, 1), (-2, 1), (3, 0), (-3, 0), (3, 1), (-3, 1), (4, 0), (4, 1),
)
MINE = {dz: LINE.index((dz, 0)) for dz in (0, 1, -1, 2, -2, 3, -3, 4)}
THEIRS = {dz: LINE.index((dz, 1)) for dz in (0, 1, -1, 2, -2, 3, -3, 4)}
TILES = (
    (0, 0, 1), (0, 1, 1), (1, 1, 1), (1, 0, 1), (0, 2, 2), (2, 2, 1), (2, 3, 2),
    (0, 3, 2), (3, 2, 1), (2, 1, 1), (2, 0, 1), (3, 1, 1), (3, 0, 1),
)
Q_TILE, K_TILE = 4 * ROWS, 4 * ROWS
NT = (((1,), (1,)), ((), ()))
TN = (((0,), (0,)), ((), ()))


def place():
    pb, ka = lax.axis_index("pb"), lax.axis_index("ka")
    x, y, z, c = (ka // 2) % 4, ka // 8, (pb // 2) * 2 + ka % 2, pb % 2
    return x, y, z, c


def device(x, y, z, c):
    return ((z // 2) * 2 + c, y * 8 + x * 2 + z % 2)


def storage(x, y, z, c):
    pb, ka = device(x, y, z, c)
    return pb * 32 + ka


def kernel(
    q_in, k_in, v_in, o_in, g_in, l_in, table_in,
    out,
    qg, kv, o_own, l_own, table, dq_acc, dk_acc, dv_acc, lrow, drow, keyid,
    dq_send, dq_recv, sib_send, sib_recv, dkv_send, dkv_recv,
    local_sem, q_ss, q_rs, kz_ss, kz_rs, kc_ss, kc_rs,
    dq_ss, dq_rs, sib_ss, sib_rs, dkv_ss, dkv_rs,
):
    x, y, z, c = place()
    other = 1 - c

    def plane_dev(i, sign):
        dx, dy = PLANE[i]
        return device((x + sign * dx + 4) % 4, (y + sign * dy + 4) % 4, z, c)

    def line_dev(dz, core):
        return device(x, y, (z + dz + 8) % 8, core)

    sibling = device(x, y, z, other)
    partners = [plane_dev(PLANE.index(at), 1) for at in ((1, 0), (3, 0), (0, 1), (0, 3), (2, 0), (0, 2))]
    partners += [line_dev(dz, c) for dz in (1, -1, 2, -2)] + [sibling]
    barrier = pltpu.get_barrier_semaphore()
    for p in partners:
        pl.semaphore_signal(barrier, inc=1, device_id=p, device_id_type=MESH)

    loads = [
        pltpu.make_async_copy(k_in, kv.at[0, 0], local_sem.at[0]),
        pltpu.make_async_copy(v_in, kv.at[1, 0], local_sem.at[1]),
        pltpu.make_async_copy(g_in, qg.at[0, pl.ds(ROWS, ROWS)], local_sem.at[2]),
        pltpu.make_async_copy(o_in, o_own, local_sem.at[3]),
        pltpu.make_async_copy(q_in, qg.at[0, pl.ds(0, ROWS)], local_sem.at[4]),
        pltpu.make_async_copy(l_in, l_own, local_sem.at[5]),
        pltpu.make_async_copy(table_in, table, local_sem.at[6]),
    ]
    for cp in loads:
        cp.start()

    def q_copy(i, held, dx, dy, sem, rows=(0, CHUNK)):
        return pltpu.make_async_remote_copy(
            src_ref=qg.at[held, pl.ds(*rows)], dst_ref=qg.at[i, pl.ds(*rows)],
            send_sem=q_ss.at[sem], recv_sem=q_rs.at[sem],
            device_id=device((x - dx + 4) % 4, (y - dy + 4) % 4, z, c), device_id_type=MESH,
        )

    at = {offset: i for i, offset in enumerate(PLANE)}
    q_cps = {}
    for offset in ((1, 0), (3, 0), (0, 1), (0, 3), (2, 0), (0, 2)):
        q_cps[at[offset]] = q_copy(at[offset], 0, *offset, at[offset])
    for dx, dy in ((1, 1), (3, 3), (1, 2), (3, 2)):
        q_cps[at[dx, dy]] = q_copy(at[dx, dy], at[0, dy], dx, 0, at[dx, dy])
    for dx, dy in ((1, 3), (3, 1), (2, 1), (2, 3)):
        q_cps[at[dx, dy]] = q_copy(at[dx, dy], at[dx, 0], 0, dy, at[dx, dy])
    far = at[2, 2]
    q_cps[far] = q_copy(far, at[0, 2], 2, 0, far, (0, 176))
    q_cps[16] = q_copy(far, at[2, 0], 0, 2, 16, (176, CHUNK - 176))

    kz_cps = {}
    for dz, (held, step) in {
        1: (0, 1), -1: (0, -1), 2: (0, 2), -2: (0, -2), 3: (1, 2), -3: (-1, -2),
    }.items():
        kz_cps[dz] = pltpu.make_async_remote_copy(
            src_ref=kv.at[:, MINE[held]], dst_ref=kv.at[:, MINE[dz]],
            send_sem=kz_ss.at[dz + 3], recv_sem=kz_rs.at[dz + 3],
            device_id=line_dev(-step, c), device_id_type=MESH,
        )
    for name, part, step in ((4, 0, 2), (5, 1, -2)):
        kz_cps[name] = pltpu.make_async_remote_copy(
            src_ref=kv.at[part, MINE[step]], dst_ref=kv.at[part, MINE[4]],
            send_sem=kz_ss.at[name + 3], recv_sem=kz_rs.at[name + 3],
            device_id=line_dev(-step, c), device_id_type=MESH,
        )
    kc_cps = {
        dz: pltpu.make_async_remote_copy(
            src_ref=kv.at[:, MINE[dz]], dst_ref=kv.at[:, THEIRS[dz]],
            send_sem=kc_ss.at[dz + 3], recv_sem=kc_rs.at[dz + 3],
            device_id=sibling, device_id_type=MESH,
        )
        for dz in MINE
    }

    for cp in loads[:2]:
        cp.wait()
    pl.semaphore_wait(barrier, len(partners))
    for dz in (1, -1):
        kz_cps[dz].start()
    kc_cps[0].start()
    for dz in (2, -2):
        kz_cps[dz].start()

    for cp in loads[2:]:
        cp.wait()
    q0, g0 = qg[0, 0:ROWS, :], qg[0, ROWS : 2 * ROWS, :]
    k0, v0 = kv[0, 0], kv[1, 0]
    prod = g0.astype(F32) * o_own[...].astype(F32)
    high = prod.astype(BF16)
    low = (prod - high.astype(F32)).astype(BF16)
    ones = jnp.ones((8, WIDTH), BF16)
    delta8 = lax.dot_general(ones, high, NT, preferred_element_type=F32)
    delta8 += lax.dot_general(ones, low, NT, preferred_element_type=F32)
    delta = delta8[0:1, :]
    lse = l_own[...] * LOG2E
    sub = lax.broadcasted_iota(jnp.int32, (8, ROWS), 0)
    both = jnp.where(sub % 2 == 0, lse, delta)
    p1 = both.astype(BF16).astype(F32)
    p2 = (both - p1).astype(BF16).astype(F32)
    p3 = both - p1 - p2
    pieces = jnp.where(sub < 2, p1, jnp.where(sub < 4, p2, jnp.where(sub < 6, p3, 0.0)))
    wide = jnp.concatenate([pieces, jnp.zeros((8, 256 - ROWS), F32)], axis=1)
    first, rest = wide[:, 0:128], wide[:, 128:256]
    lane = lax.broadcasted_iota(jnp.int32, (8, 128), 1)
    second = jnp.where(
        lane < 48, pltpu.roll(first, 48, 1), pltpu.roll(rest, 48, 1)
    )
    keep = lane < BLK
    stats = jnp.concatenate(
        [jnp.where(keep, first, 0.0), jnp.where(keep, second, 0.0)], axis=0
    )
    qg[0, 2 * ROWS : CHUNK, :] = stats.astype(BF16)

    for offset in ((1, 0), (3, 0), (0, 1), (0, 3), (2, 0), (0, 2)):
        q_cps[at[offset]].start()
    dq_acc[...] = jnp.zeros_like(dq_acc)
    dk_acc[...] = jnp.zeros_like(dk_acc)
    dv_acc[...] = jnp.zeros_like(dv_acc)

    row = lax.broadcasted_iota(jnp.int32, (ROWS, ROWS), 0)
    col = lax.broadcasted_iota(jnp.int32, (ROWS, ROWS), 1)
    seen = (row <= col) & ((row >= BLK) == (col >= BLK))
    s0 = lax.dot_general(k0, q0, NT, preferred_element_type=F32)
    e0 = jnp.exp2(jnp.where(seen, s0 * TO_EXP2 - lse, -HIDDEN))
    dp0 = lax.dot_general(v0, g0, NT, preferred_element_type=F32)
    ds0 = (e0 * (dp0 - delta)).astype(BF16)
    dq_acc[0:ROWS, :] = lax.dot_general(ds0, k0, TN, preferred_element_type=F32)
    dk_acc[0:ROWS, :] = jnp.dot(ds0, q0, preferred_element_type=F32)
    dv_acc[0:ROWS, :] = jnp.dot(e0.astype(BF16), g0, preferred_element_type=F32)

    for r in range(32):
        dz, h = LINE[r // 2]
        entry = storage(x, y, (z + dz + 8) % 8, c if h == 0 else other) * 2 + r % 2
        keyid[r : r + 1, :] = jnp.full((1, 128), table[entry], jnp.int32)

    def rows_of(t):
        blocks = []
        for i in range(4 * t, 4 * t + 4):
            st = qg[i, 2 * ROWS : CHUNK, :].astype(F32)
            dx, dy = PLANE[i]
            entry = storage((x + dx) % 4, (y + dy) % 4, z, c) * 2
            blocks += [(st[0:8, :], table[entry]), (st[8:16, :], table[entry + 1])]
        for j in range(5):
            acc = jnp.zeros((8, 128), F32)
            ids = jnp.zeros((8, 128), jnp.int32)
            for r, (st, entry) in enumerate(blocks):
                shift = BLK * r - 128 * j
                if shift <= -BLK or shift >= 128:
                    continue
                here = (lane >= max(shift, 0)) & (lane < min(128, shift + BLK))
                moved = st if shift % 128 == 0 else pltpu.roll(st, shift % 128, 1)
                acc = jnp.where(here, moved, acc)
                ids = jnp.where(here, entry, ids)
            lr = acc[0:1, :] + acc[2:3, :] + acc[4:5, :]
            dr = acc[1:2, :] + acc[3:4, :] + acc[5:6, :]
            cols = slice(Q_TILE * t + 128 * j, Q_TILE * t + 128 * (j + 1))
            drow[:, cols] = jnp.broadcast_to(dr, (8, 128))
            lb = jnp.broadcast_to(lr, (8, 128))
            for u in range(4):
                lrow[8 * u : 8 * u + 8, cols] = jnp.where(
                    ids > keyid[8 * u : 8 * u + 8, :], lb, HIDDEN
                )

    def tile(qi, ki, wide):
        n_queries = wide * Q_TILE
        qs = pl.ds(qi * Q_TILE, n_queries)
        ks = pl.ds(ki * K_TILE, K_TILE)
        q = qg[pl.ds(qi * 4, wide * 4), 0:ROWS, :].reshape(n_queries, WIDTH)
        g = qg[pl.ds(qi * 4, wide * 4), ROWS : 2 * ROWS, :].reshape(n_queries, WIDTH)
        k = kv[0, pl.ds(ki * 4, 4), :, :].reshape(K_TILE, WIDTH)
        v = kv[1, pl.ds(ki * 4, 4), :, :].reshape(K_TILE, WIDTH)
        s = lax.dot_general(k, q, NT, preferred_element_type=F32)
        dp = lax.dot_general(v, g, NT, preferred_element_type=F32)
        lr = lrow[pl.ds(ki * 8, 8), qs]
        bias = jnp.broadcast_to(lr[:, None, :], (8, BLK, n_queries)).reshape(K_TILE, n_queries)
        p = jnp.exp2(s * TO_EXP2 - bias)
        ds = (p * (dp - drow[0:1, qs])).astype(BF16)
        dv_acc[ks, :] += jnp.dot(p.astype(BF16), g, preferred_element_type=F32)
        dk_acc[ks, :] += jnp.dot(ds, q, preferred_element_type=F32)
        dq_acc[qs, :] += lax.dot_general(ds, k, TN, preferred_element_type=F32)

    dq_cps = {
        i: pltpu.make_async_remote_copy(
            src_ref=dq_send.at[i], dst_ref=dq_recv.at[i],
            send_sem=dq_ss.at[i], recv_sem=dq_rs.at[i],
            device_id=plane_dev(i, 1), device_id_type=MESH,
        )
        for i in range(1, 16)
    }
    sib_cps = {
        dz: pltpu.make_async_remote_copy(
            src_ref=sib_send.at[dz + 3], dst_ref=sib_recv.at[dz + 3],
            send_sem=sib_ss.at[dz + 3], recv_sem=sib_rs.at[dz + 3],
            device_id=sibling, device_id_type=MESH,
        )
        for dz in MINE
    }
    dkv_cps = {
        dz: pltpu.make_async_remote_copy(
            src_ref=dkv_send.at[dz + 3], dst_ref=dkv_recv.at[dz + 3],
            send_sem=dkv_ss.at[dz + 3], recv_sem=dkv_rs.at[dz + 3],
            device_id=line_dev(step, c), device_id_type=MESH,
        )
        for dz, step in {1: 1, -1: -1, 2: 2, -2: -2, 3: 2, -3: -2}.items()
    }
    for name, part, step in ((4, 0, 2), (5, 1, -2)):
        dkv_cps[name] = pltpu.make_async_remote_copy(
            src_ref=dkv_send.at[7, part], dst_ref=dkv_recv.at[7, part],
            send_sem=dkv_ss.at[name + 3], recv_sem=dkv_rs.at[name + 3],
            device_id=line_dev(step, c), device_id_type=MESH,
        )

    def queries_out(t):
        for i in range(4 * t, 4 * t + 4):
            if i > 0:
                dq_send[i] = dq_acc[i * ROWS : (i + 1) * ROWS, :].astype(BF16)
                dq_cps[i].start()

    def part(acc, i):
        return acc[i * ROWS : (i + 1) * ROWS, :]

    def to_sibling(dz):
        sib_send[dz + 3, 0] = part(dk_acc, THEIRS[dz]).astype(BF16)
        sib_send[dz + 3, 1] = part(dv_acc, THEIRS[dz]).astype(BF16)
        sib_cps[dz].start()

    def chip_sum(dz):
        sib_cps[dz].wait_recv()
        a = part(dk_acc, MINE[dz]) + sib_recv[dz + 3, 0].astype(F32)
        b = part(dv_acc, MINE[dz]) + sib_recv[dz + 3, 1].astype(F32)
        return a, b

    def to_owner(dz):
        a, b = chip_sum(dz)
        if dz in (1, -1):
            dkv_cps[3 * dz].wait_recv()
            a = a + dkv_recv[3 * dz + 3, 0].astype(F32)
            b = b + dkv_recv[3 * dz + 3, 1].astype(F32)
        if dz == 2:
            dkv_cps[4].wait_recv()
            a = a + dkv_recv[7, 0].astype(F32)
        if dz == -2:
            dkv_cps[5].wait_recv()
            b = b + dkv_recv[7, 1].astype(F32)
        dkv_send[dz + 3, 0] = a.astype(BF16)
        dkv_send[dz + 3, 1] = b.astype(BF16)
        dkv_cps[dz].start()
        if dz == 4:
            dkv_cps[5].start()

    def before(n):
        if n == 0:
            for offset in ((1, 0), (3, 0), (0, 1), (0, 3)):
                q_cps[at[offset]].wait_recv()
            for offset in ((1, 1), (3, 3), (1, 3), (3, 1)):
                q_cps[at[offset]].start()
            for dz in (1, -1):
                kz_cps[dz].wait_recv()
                kz_cps[3 * dz].start()
                kc_cps[dz].start()
            rows_of(0)
            kc_cps[0].wait_recv()
        if n == 1:
            for dz in (2, -2):
                kz_cps[dz].wait_recv()
                kz_cps[4 if dz == 2 else 5].start()
                kc_cps[dz].start()
            for offset in ((2, 0), (0, 2)):
                q_cps[at[offset]].wait_recv()
            for i in (at[1, 2], at[2, 1], at[3, 2], at[2, 3], far, 16):
                q_cps[i].start()
            kc_cps[1].wait_recv()
            kc_cps[-1].wait_recv()
        if n == 2:
            q_cps[at[1, 1]].wait_recv()
            rows_of(1)
        if n == 4:
            for dz in (3, -3):
                kz_cps[dz].wait_recv()
                kc_cps[dz].start()
            kc_cps[2].wait_recv()
            kc_cps[-2].wait_recv()
        if n == 5:
            kz_cps[4].wait_recv()
            kz_cps[5].wait_recv()
            kc_cps[4].start()
            for i in (8, 9, 10, 11, 16):
                q_cps[i].wait_recv()
            rows_of(2)
        if n == 6:
            for i in (12, 13, 14, 15):
                q_cps[i].wait_recv()
            rows_of(3)
            for dz in (3, -3, 4):
                kc_cps[dz].wait_recv()
        if n == 8:
            for dz in (4, 3, -3):
                to_sibling(dz)
            queries_out(0)
            queries_out(1)
        if n == 9:
            for dz in (4, 3, -3):
                to_owner(dz)
            to_sibling(2)
            to_sibling(-2)
        if n == 11:
            queries_out(2)
        if n == 12:
            to_sibling(1)
            to_sibling(-1)

    for n, (qi, ki, wide) in enumerate(TILES):
        before(n)
        tile(qi, ki, wide)

    to_sibling(0)
    queries_out(3)
    for dz in (2, -2, 1, -1):
        to_owner(dz)

    a, b = chip_sum(0)
    total = dq_acc[0:ROWS, :]
    for i in range(1, 16):
        dq_cps[i].wait_recv()
        total = total + dq_recv[i].astype(F32)
    out[0] = (total * SCALE).astype(BF16)
    for dz in (2, -2, 1, -1):
        dkv_cps[dz].wait_recv()
        a = a + dkv_recv[dz + 3, 0].astype(F32)
        b = b + dkv_recv[dz + 3, 1].astype(F32)
    out[1] = (a * SCALE).astype(BF16)
    out[2] = b.astype(BF16)

    for group in (q_cps, kz_cps, kc_cps, dq_cps, dkv_cps, sib_cps):
        for cp in group.values():
            cp.wait_send()


def per_device(queries, keys_in, values_in, outputs_saved, out_grad, log_sum, block_table):
    hbm = pl.BlockSpec(memory_space=pl.ANY)
    vmem = pl.BlockSpec(memory_space=pltpu.VMEM)
    dma = pltpu.SemaphoreType.DMA
    sums = pl.pallas_call(
        kernel,
        out_shape=jax.ShapeDtypeStruct((3, ROWS, WIDTH), BF16),
        in_specs=[hbm] * 7,
        out_specs=vmem,
        scratch_shapes=[
            pltpu.VMEM((16, CHUNK, WIDTH), BF16),
            pltpu.VMEM((2, 16, ROWS, WIDTH), BF16),
            pltpu.VMEM((ROWS, WIDTH), BF16),
            pltpu.VMEM((1, ROWS), F32),
            pltpu.SMEM((512,), jnp.int32),
            pltpu.VMEM((16 * ROWS, WIDTH), F32),
            pltpu.VMEM((16 * ROWS, WIDTH), F32),
            pltpu.VMEM((16 * ROWS, WIDTH), F32),
            pltpu.VMEM((32, 16 * ROWS), F32),
            pltpu.VMEM((8, 16 * ROWS), F32),
            pltpu.VMEM((32, 128), jnp.int32),
            pltpu.VMEM((16, ROWS, WIDTH), BF16),
            pltpu.VMEM((16, ROWS, WIDTH), BF16),
            pltpu.VMEM((8, 2, ROWS, WIDTH), BF16),
            pltpu.VMEM((8, 2, ROWS, WIDTH), BF16),
            pltpu.VMEM((8, 2, ROWS, WIDTH), BF16),
            pltpu.VMEM((8, 2, ROWS, WIDTH), BF16),
            dma((7,)), dma((17,)), dma((17,)), dma((9,)), dma((9,)), dma((8,)), dma((8,)),
            dma((16,)), dma((16,)), dma((8,)), dma((8,)), dma((9,)), dma((9,)),
        ],
        compiler_params=pltpu.CompilerParams(
            collective_id=0, has_side_effects=True, vmem_limit_bytes=60 << 20
        ),
    )(
        queries, keys_in, values_in, outputs_saved, out_grad,
        log_sum.reshape(1, ROWS), block_table,
    )
    return tuple(sums[i] for i in range(3))


def solution(mesh):
    rows = P(("pb", "ka"), None)
    return jax.shard_map(
        per_device,
        mesh=mesh,
        in_specs=(rows, rows, rows, rows, rows, P(("pb", "ka")), P()),
        out_specs=(rows, rows, rows),
        check_vma=False,
    )
```

```python
import math

import jax
import jax.numpy as jnp
from jax import lax
from jax.experimental import pallas as pl
from jax.experimental.pallas import tpu as pltpu
from jax.sharding import PartitionSpec as P

MESH = pl.DeviceIdType.MESH
F32, BF16 = jnp.float32, jnp.bfloat16
ROWS = 160
BLK = 80
WIDTH = 128
SCALE = 1.0 / math.sqrt(WIDTH)
TO_EXP2 = SCALE * math.log2(math.e)
LOG2E = math.log2(math.e)
HIDDEN = 1e30
CHUNK = 336
PLANE = (
    (0, 0), (1, 0), (3, 0), (0, 1), (0, 3), (2, 0), (0, 2), (1, 1),
    (2, 2), (2, 1), (2, 3), (1, 2), (3, 2), (3, 3), (1, 3), (3, 1),
)
LINE = (
    (0, 0), (1, 0), (-1, 0), (0, 1), (1, 1), (-1, 1), (2, 0), (-2, 0),
    (2, 1), (-2, 1), (3, 0), (-3, 0), (3, 1), (-3, 1), (4, 0), (4, 1),
)
MINE = {dz: LINE.index((dz, 0)) for dz in (0, 1, -1, 2, -2, 3, -3, 4)}
THEIRS = {dz: LINE.index((dz, 1)) for dz in (0, 1, -1, 2, -2, 3, -3, 4)}
TILES = (
    (0, 0, 1), (0, 1, 1), (1, 1, 1), (1, 0, 1), (0, 2, 2), (2, 2, 1), (2, 3, 2),
    (0, 3, 2), (3, 2, 1), (2, 1, 1), (2, 0, 1), (3, 1, 1), (3, 0, 1),
)
Q_TILE, K_TILE = 4 * ROWS, 4 * ROWS
NT = (((1,), (1,)), ((), ()))
TN = (((0,), (0,)), ((), ()))


def place():
    pb, ka = lax.axis_index("pb"), lax.axis_index("ka")
    x, y, z, c = (ka // 2) % 4, ka // 8, (pb // 2) * 2 + ka % 2, pb % 2
    return x, y, z, c


def device(x, y, z, c):
    return ((z // 2) * 2 + c, y * 8 + x * 2 + z % 2)


def storage(x, y, z, c):
    pb, ka = device(x, y, z, c)
    return pb * 32 + ka


def kernel(
    q_in, k_in, v_in, o_in, g_in, l_in, table_in,
    out_hbm,
    out, qg, kv, o_own, l_own, table, dq_acc, dk_acc, dv_acc, lrow, drow, keyid,
    dq_send, dq_recv, sib_send, sib_recv, dkv_send, dkv_recv,
    local_sem, q_ss, q_rs, kz_ss, kz_rs, kc_ss, kc_rs,
    dq_ss, dq_rs, sib_ss, sib_rs, dkv_ss, dkv_rs,
):
    x, y, z, c = place()
    other = 1 - c

    def plane_dev(i, sign):
        dx, dy = PLANE[i]
        return device((x + sign * dx + 4) % 4, (y + sign * dy + 4) % 4, z, c)

    def line_dev(dz, core):
        return device(x, y, (z + dz + 8) % 8, core)

    sibling = device(x, y, z, other)
    partners = [plane_dev(PLANE.index(at), 1) for at in ((1, 0), (3, 0), (0, 1), (0, 3), (2, 0), (0, 2))]
    partners += [line_dev(dz, c) for dz in (1, -1, 2, -2)] + [sibling]
    barrier = pltpu.get_barrier_semaphore()
    for p in partners:
        pl.semaphore_signal(barrier, inc=1, device_id=p, device_id_type=MESH)

    loads = [
        pltpu.make_async_copy(k_in, kv.at[0, 0], local_sem.at[0]),
        pltpu.make_async_copy(v_in, kv.at[1, 0], local_sem.at[1]),
        pltpu.make_async_copy(g_in, qg.at[0, pl.ds(ROWS, ROWS)], local_sem.at[2]),
        pltpu.make_async_copy(o_in, o_own, local_sem.at[3]),
        pltpu.make_async_copy(q_in, qg.at[0, pl.ds(0, ROWS)], local_sem.at[4]),
        pltpu.make_async_copy(l_in, l_own, local_sem.at[5]),
        pltpu.make_async_copy(table_in, table, local_sem.at[6]),
    ]
    for cp in loads:
        cp.start()

    def q_copy(i, held, dx, dy, sem, rows=(0, CHUNK)):
        return pltpu.make_async_remote_copy(
            src_ref=qg.at[held, pl.ds(*rows)], dst_ref=qg.at[i, pl.ds(*rows)],
            send_sem=q_ss.at[sem], recv_sem=q_rs.at[sem],
            device_id=device((x - dx + 4) % 4, (y - dy + 4) % 4, z, c), device_id_type=MESH,
        )

    at = {offset: i for i, offset in enumerate(PLANE)}
    q_cps = {}
    for offset in ((1, 0), (3, 0), (0, 1), (0, 3), (2, 0), (0, 2)):
        q_cps[at[offset]] = q_copy(at[offset], 0, *offset, at[offset])
    for dx, dy in ((1, 1), (3, 3), (1, 2), (3, 2)):
        q_cps[at[dx, dy]] = q_copy(at[dx, dy], at[0, dy], dx, 0, at[dx, dy])
    for dx, dy in ((1, 3), (3, 1), (2, 1), (2, 3)):
        q_cps[at[dx, dy]] = q_copy(at[dx, dy], at[dx, 0], 0, dy, at[dx, dy])
    far = at[2, 2]
    q_cps[far] = q_copy(far, at[0, 2], 2, 0, far, (0, 176))
    q_cps[16] = q_copy(far, at[2, 0], 0, 2, 16, (176, CHUNK - 176))

    kz_cps = {}
    for dz, (held, step) in {
        1: (0, 1), -1: (0, -1), 2: (0, 2), -2: (0, -2), 3: (1, 2), -3: (-1, -2),
    }.items():
        kz_cps[dz] = pltpu.make_async_remote_copy(
            src_ref=kv.at[:, MINE[held]], dst_ref=kv.at[:, MINE[dz]],
            send_sem=kz_ss.at[dz + 3], recv_sem=kz_rs.at[dz + 3],
            device_id=line_dev(-step, c), device_id_type=MESH,
        )
    for name, part, step in ((4, 0, 2), (5, 1, -2)):
        kz_cps[name] = pltpu.make_async_remote_copy(
            src_ref=kv.at[part, MINE[step]], dst_ref=kv.at[part, MINE[4]],
            send_sem=kz_ss.at[name + 3], recv_sem=kz_rs.at[name + 3],
            device_id=line_dev(-step, c), device_id_type=MESH,
        )
    kc_cps = {
        dz: pltpu.make_async_remote_copy(
            src_ref=kv.at[:, MINE[dz]], dst_ref=kv.at[:, THEIRS[dz]],
            send_sem=kc_ss.at[dz + 3], recv_sem=kc_rs.at[dz + 3],
            device_id=sibling, device_id_type=MESH,
        )
        for dz in MINE
    }

    for cp in loads[:2]:
        cp.wait()
    pl.semaphore_wait(barrier, len(partners))
    for dz in (1, -1):
        kz_cps[dz].start()
    kc_cps[0].start()
    for dz in (2, -2):
        kz_cps[dz].start()

    for cp in loads[2:]:
        cp.wait()
    q0, g0 = qg[0, 0:ROWS, :], qg[0, ROWS : 2 * ROWS, :]
    k0, v0 = kv[0, 0], kv[1, 0]
    prod = g0.astype(F32) * o_own[...].astype(F32)
    high = prod.astype(BF16)
    low = (prod - high.astype(F32)).astype(BF16)
    ones = jnp.ones((8, WIDTH), BF16)
    delta8 = lax.dot_general(ones, high, NT, preferred_element_type=F32)
    delta8 += lax.dot_general(ones, low, NT, preferred_element_type=F32)
    delta = delta8[0:1, :]
    lse = l_own[...] * LOG2E
    sub = lax.broadcasted_iota(jnp.int32, (8, ROWS), 0)
    both = jnp.where(sub % 2 == 0, lse, delta)
    p1 = both.astype(BF16).astype(F32)
    p2 = (both - p1).astype(BF16).astype(F32)
    p3 = both - p1 - p2
    pieces = jnp.where(sub < 2, p1, jnp.where(sub < 4, p2, jnp.where(sub < 6, p3, 0.0)))
    wide = jnp.concatenate([pieces, jnp.zeros((8, 256 - ROWS), F32)], axis=1)
    first, rest = wide[:, 0:128], wide[:, 128:256]
    lane = lax.broadcasted_iota(jnp.int32, (8, 128), 1)
    second = jnp.where(
        lane < 48, pltpu.roll(first, 48, 1), pltpu.roll(rest, 48, 1)
    )
    keep = lane < BLK
    stats = jnp.concatenate(
        [jnp.where(keep, first, 0.0), jnp.where(keep, second, 0.0)], axis=0
    )
    qg[0, 2 * ROWS : CHUNK, :] = stats.astype(BF16)

    for offset in ((1, 0), (3, 0), (0, 1), (0, 3), (2, 0), (0, 2)):
        q_cps[at[offset]].start()
    dq_acc[...] = jnp.zeros_like(dq_acc)
    dk_acc[...] = jnp.zeros_like(dk_acc)
    dv_acc[...] = jnp.zeros_like(dv_acc)

    row = lax.broadcasted_iota(jnp.int32, (ROWS, ROWS), 0)
    col = lax.broadcasted_iota(jnp.int32, (ROWS, ROWS), 1)
    seen = (row <= col) & ((row >= BLK) == (col >= BLK))
    s0 = lax.dot_general(k0, q0, NT, preferred_element_type=F32)
    e0 = jnp.exp2(jnp.where(seen, s0 * TO_EXP2 - lse, -HIDDEN))
    dp0 = lax.dot_general(v0, g0, NT, preferred_element_type=F32)
    ds0 = (e0 * (dp0 - delta)).astype(BF16)
    dq_acc[0:ROWS, :] = lax.dot_general(ds0, k0, TN, preferred_element_type=F32)
    dk_acc[0:ROWS, :] = jnp.dot(ds0, q0, preferred_element_type=F32)
    dv_acc[0:ROWS, :] = jnp.dot(e0.astype(BF16), g0, preferred_element_type=F32)

    for r in range(32):
        dz, h = LINE[r // 2]
        entry = storage(x, y, (z + dz + 8) % 8, c if h == 0 else other) * 2 + r % 2
        keyid[r : r + 1, :] = jnp.full((1, 128), table[entry], jnp.int32)

    def rows_of(t):
        blocks = []
        for i in range(4 * t, 4 * t + 4):
            st = qg[i, 2 * ROWS : CHUNK, :].astype(F32)
            dx, dy = PLANE[i]
            entry = storage((x + dx) % 4, (y + dy) % 4, z, c) * 2
            blocks += [(st[0:8, :], table[entry]), (st[8:16, :], table[entry + 1])]
        for j in range(5):
            acc = jnp.zeros((8, 128), F32)
            ids = jnp.zeros((8, 128), jnp.int32)
            for r, (st, entry) in enumerate(blocks):
                shift = BLK * r - 128 * j
                if shift <= -BLK or shift >= 128:
                    continue
                here = (lane >= max(shift, 0)) & (lane < min(128, shift + BLK))
                moved = st if shift % 128 == 0 else pltpu.roll(st, shift % 128, 1)
                acc = jnp.where(here, moved, acc)
                ids = jnp.where(here, entry, ids)
            lr = acc[0:1, :] + acc[2:3, :] + acc[4:5, :]
            dr = acc[1:2, :] + acc[3:4, :] + acc[5:6, :]
            cols = slice(Q_TILE * t + 128 * j, Q_TILE * t + 128 * (j + 1))
            drow[:, cols] = jnp.broadcast_to(dr, (8, 128))
            lb = jnp.broadcast_to(lr, (8, 128))
            for u in range(4):
                lrow[8 * u : 8 * u + 8, cols] = jnp.where(
                    ids > keyid[8 * u : 8 * u + 8, :], lb, HIDDEN
                )

    def tile(qi, ki, wide):
        n_queries = wide * Q_TILE
        qs = pl.ds(qi * Q_TILE, n_queries)
        ks = pl.ds(ki * K_TILE, K_TILE)
        q = qg[pl.ds(qi * 4, wide * 4), 0:ROWS, :].reshape(n_queries, WIDTH)
        g = qg[pl.ds(qi * 4, wide * 4), ROWS : 2 * ROWS, :].reshape(n_queries, WIDTH)
        k = kv[0, pl.ds(ki * 4, 4), :, :].reshape(K_TILE, WIDTH)
        v = kv[1, pl.ds(ki * 4, 4), :, :].reshape(K_TILE, WIDTH)
        s = lax.dot_general(k, q, NT, preferred_element_type=F32)
        dp = lax.dot_general(v, g, NT, preferred_element_type=F32)
        lr = lrow[pl.ds(ki * 8, 8), qs]
        bias = jnp.broadcast_to(lr[:, None, :], (8, BLK, n_queries)).reshape(K_TILE, n_queries)
        p = jnp.exp2(s * TO_EXP2 - bias)
        ds = (p * (dp - drow[0:1, qs])).astype(BF16)
        dv_acc[ks, :] += jnp.dot(p.astype(BF16), g, preferred_element_type=F32)
        dk_acc[ks, :] += jnp.dot(ds, q, preferred_element_type=F32)
        dq_acc[qs, :] += lax.dot_general(ds, k, TN, preferred_element_type=F32)

    dq_cps = {
        i: pltpu.make_async_remote_copy(
            src_ref=dq_send.at[i], dst_ref=dq_recv.at[i],
            send_sem=dq_ss.at[i], recv_sem=dq_rs.at[i],
            device_id=plane_dev(i, 1), device_id_type=MESH,
        )
        for i in range(1, 16)
    }
    sib_cps = {
        dz: pltpu.make_async_remote_copy(
            src_ref=sib_send.at[dz + 3], dst_ref=sib_recv.at[dz + 3],
            send_sem=sib_ss.at[dz + 3], recv_sem=sib_rs.at[dz + 3],
            device_id=sibling, device_id_type=MESH,
        )
        for dz in MINE
    }
    dkv_cps = {
        dz: pltpu.make_async_remote_copy(
            src_ref=dkv_send.at[dz + 3], dst_ref=dkv_recv.at[dz + 3],
            send_sem=dkv_ss.at[dz + 3], recv_sem=dkv_rs.at[dz + 3],
            device_id=line_dev(step, c), device_id_type=MESH,
        )
        for dz, step in {1: 1, -1: -1, 2: 2, -2: -2, 3: 2, -3: -2}.items()
    }
    for name, part, step in ((4, 0, 2), (5, 1, -2)):
        dkv_cps[name] = pltpu.make_async_remote_copy(
            src_ref=dkv_send.at[7, part], dst_ref=dkv_recv.at[7, part],
            send_sem=dkv_ss.at[name + 3], recv_sem=dkv_rs.at[name + 3],
            device_id=line_dev(step, c), device_id_type=MESH,
        )

    def queries_out(t):
        for i in range(4 * t, 4 * t + 4):
            if i > 0:
                dq_send[i] = dq_acc[i * ROWS : (i + 1) * ROWS, :].astype(BF16)
                dq_cps[i].start()

    def part(acc, i):
        return acc[i * ROWS : (i + 1) * ROWS, :]

    def to_sibling(dz):
        sib_send[dz + 3, 0] = part(dk_acc, THEIRS[dz]).astype(BF16)
        sib_send[dz + 3, 1] = part(dv_acc, THEIRS[dz]).astype(BF16)
        sib_cps[dz].start()

    def chip_sum(dz):
        sib_cps[dz].wait_recv()
        a = part(dk_acc, MINE[dz]) + sib_recv[dz + 3, 0].astype(F32)
        b = part(dv_acc, MINE[dz]) + sib_recv[dz + 3, 1].astype(F32)
        return a, b

    def to_owner(dz):
        a, b = chip_sum(dz)
        if dz in (1, -1):
            dkv_cps[3 * dz].wait_recv()
            a = a + dkv_recv[3 * dz + 3, 0].astype(F32)
            b = b + dkv_recv[3 * dz + 3, 1].astype(F32)
        if dz == 2:
            dkv_cps[4].wait_recv()
            a = a + dkv_recv[7, 0].astype(F32)
        if dz == -2:
            dkv_cps[5].wait_recv()
            b = b + dkv_recv[7, 1].astype(F32)
        dkv_send[dz + 3, 0] = a.astype(BF16)
        dkv_send[dz + 3, 1] = b.astype(BF16)
        dkv_cps[dz].start()
        if dz == 4:
            dkv_cps[5].start()

    def before(n):
        if n == 0:
            for offset in ((1, 0), (3, 0), (0, 1), (0, 3)):
                q_cps[at[offset]].wait_recv()
            for offset in ((1, 1), (3, 3), (1, 3), (3, 1)):
                q_cps[at[offset]].start()
            for dz in (1, -1):
                kz_cps[dz].wait_recv()
                kz_cps[3 * dz].start()
                kc_cps[dz].start()
            rows_of(0)
            kc_cps[0].wait_recv()
        if n == 1:
            for dz in (2, -2):
                kz_cps[dz].wait_recv()
                kz_cps[4 if dz == 2 else 5].start()
                kc_cps[dz].start()
            for offset in ((2, 0), (0, 2)):
                q_cps[at[offset]].wait_recv()
            for i in (at[1, 2], at[2, 1], at[3, 2], at[2, 3], far, 16):
                q_cps[i].start()
            kc_cps[1].wait_recv()
            kc_cps[-1].wait_recv()
        if n == 2:
            q_cps[at[1, 1]].wait_recv()
            rows_of(1)
        if n == 4:
            for dz in (3, -3):
                kz_cps[dz].wait_recv()
                kc_cps[dz].start()
            kc_cps[2].wait_recv()
            kc_cps[-2].wait_recv()
        if n == 5:
            kz_cps[4].wait_recv()
            kz_cps[5].wait_recv()
            kc_cps[4].start()
            for i in (8, 9, 10, 11, 16):
                q_cps[i].wait_recv()
            rows_of(2)
        if n == 6:
            for i in (12, 13, 14, 15):
                q_cps[i].wait_recv()
            rows_of(3)
            for dz in (3, -3, 4):
                kc_cps[dz].wait_recv()
        if n == 8:
            for dz in (4, 3, -3):
                to_sibling(dz)
            queries_out(0)
            queries_out(1)
        if n == 9:
            for dz in (4, 3, -3):
                to_owner(dz)
            to_sibling(2)
            to_sibling(-2)
        if n == 11:
            queries_out(2)
        if n == 12:
            to_sibling(1)
            to_sibling(-1)

    for n, (qi, ki, wide) in enumerate(TILES):
        before(n)
        tile(qi, ki, wide)

    to_sibling(0)
    queries_out(3)
    for dz in (2, -2, 1, -1):
        to_owner(dz)

    a, b = chip_sum(0)
    total = dq_acc[0:ROWS, :]
    for i in range(1, 16):
        dq_cps[i].wait_recv()
        total = total + dq_recv[i].astype(F32)
    out[0] = (total * SCALE).astype(BF16)
    first_out = pltpu.make_async_copy(out.at[0], out_hbm.at[0], local_sem.at[7])
    first_out.start()
    for dz in (2, -2, 1, -1):
        dkv_cps[dz].wait_recv()
        a = a + dkv_recv[dz + 3, 0].astype(F32)
        b = b + dkv_recv[dz + 3, 1].astype(F32)
    out[1] = (a * SCALE).astype(BF16)
    out[2] = b.astype(BF16)
    rest_out = pltpu.make_async_copy(out.at[pl.ds(1, 2)], out_hbm.at[pl.ds(1, 2)], local_sem.at[8])
    rest_out.start()

    for group in (q_cps, kz_cps, kc_cps, dq_cps, dkv_cps, sib_cps):
        for cp in group.values():
            cp.wait_send()
    first_out.wait()
    rest_out.wait()


def per_device(queries, keys_in, values_in, outputs_saved, out_grad, log_sum, block_table):
    hbm = pl.BlockSpec(memory_space=pl.ANY)
    dma = pltpu.SemaphoreType.DMA
    sums = pl.pallas_call(
        kernel,
        out_shape=jax.ShapeDtypeStruct((3, ROWS, WIDTH), BF16),
        in_specs=[hbm] * 7,
        out_specs=hbm,
        scratch_shapes=[
            pltpu.VMEM((3, ROWS, WIDTH), BF16),
            pltpu.VMEM((16, CHUNK, WIDTH), BF16),
            pltpu.VMEM((2, 16, ROWS, WIDTH), BF16),
            pltpu.VMEM((ROWS, WIDTH), BF16),
            pltpu.VMEM((1, ROWS), F32),
            pltpu.SMEM((512,), jnp.int32),
            pltpu.VMEM((16 * ROWS, WIDTH), F32),
            pltpu.VMEM((16 * ROWS, WIDTH), F32),
            pltpu.VMEM((16 * ROWS, WIDTH), F32),
            pltpu.VMEM((32, 16 * ROWS), F32),
            pltpu.VMEM((8, 16 * ROWS), F32),
            pltpu.VMEM((32, 128), jnp.int32),
            pltpu.VMEM((16, ROWS, WIDTH), BF16),
            pltpu.VMEM((16, ROWS, WIDTH), BF16),
            pltpu.VMEM((8, 2, ROWS, WIDTH), BF16),
            pltpu.VMEM((8, 2, ROWS, WIDTH), BF16),
            pltpu.VMEM((8, 2, ROWS, WIDTH), BF16),
            pltpu.VMEM((8, 2, ROWS, WIDTH), BF16),
            dma((9,)), dma((17,)), dma((17,)), dma((9,)), dma((9,)), dma((8,)), dma((8,)),
            dma((16,)), dma((16,)), dma((8,)), dma((8,)), dma((9,)), dma((9,)),
        ],
        compiler_params=pltpu.CompilerParams(
            collective_id=0, has_side_effects=True, vmem_limit_bytes=60 << 20
        ),
    )(
        queries, keys_in, values_in, outputs_saved, out_grad,
        log_sum.reshape(1, ROWS), block_table,
    )
    return tuple(sums[i] for i in range(3))


def solution(mesh):
    rows = P(("pb", "ka"), None)
    return jax.shard_map(
        per_device,
        mesh=mesh,
        in_specs=(rows, rows, rows, rows, rows, P(("pb", "ka")), P()),
        out_specs=(rows, rows, rows),
        check_vma=False,
    )
```
